512 devices in a mesh: dp: 32 (over y_lo, z), tensor: 16 (over x, y_hi, core).
Axes of the slice: x: 4, y: 4 (y_hi: 2, y_lo: 2; y = y_hi * 2 + y_lo), z: 16, core: 2. Of those that a mesh axis runs over, the one named last changes fastest.
Arguments:
- hidden: bfloat16 [8192, 14336], P('dp', 'tensor'), may hold values from -6 to 6
- tenant_ids: int32 [16], replicated, may hold values from 0 to 3
- base_weight: bfloat16 [14336, 4096], P('tensor', 'dp'), may hold values from -0.09375 to 0.09375
- adapter_in: bfloat16 [14336, 128], P('tensor'), may hold values from -0.10857488 to 0.10857488
- adapter_out: bfloat16 [128, 4096], P(None, 'tensor'), may hold values from -0.5 to 0.5
- magnitude: float32 [4, 4096], P(None, 'tensor'), may hold values from 0.5 to 2
- cotangent: bfloat16 [8192, 4096], P('dp', 'tensor'), may hold values from -6 to 6
Outputs:
- adapted: bfloat16 [8192, 4096], P('dp', 'tensor')
- input_grad: bfloat16 [8192, 14336], P('dp', 'tensor')
- grad_in: float32 [14336, 128], P('tensor')
- grad_out: float32 [128, 4096], P(None, 'tensor')
- grad_mag: float32 [4, 4096], P(None, 'tensor')
The draws below stay inside these ranges and needn't reach their ends.
Inputs may be any that keep to these rules, and one draw needn't show every extreme that they name: `tenant_ids`: the tenant of each block of 512 consecutive tokens.
All inputs are finite; a program needn't handle non-finite values.
Results may differ from the reference program's by a relative error of at most 0.0049.
Values may be sent and summed in bfloat16 or wider, within the bound.
A program may use at most 64 MiB of HBM per device.

```python
import math
import jax
import jax.numpy as jnp
from jax import lax

D = 4096
FF = 14336
R = 32
K = 4
BLOCK = 512
TOKENS = 8192
BLOCKS = 16
ADAPT = 128


def draw_adapter_in(key, part):
    key = jax.random.fold_in(key, 11)
    key_own, key_shared, key_coef = jax.random.split(key, 3)
    own = jnp.clip(jax.random.normal(key_own, (FF, K * R), jnp.float32), -4.0, 4.0)
    shared = jnp.clip(jax.random.normal(key_shared, (FF, K), jnp.float32), -4.0, 4.0)
    coefs = jax.random.uniform(key_coef, (K * R,), jnp.float32, 0.5, 1.5)
    shared_cols = jnp.repeat(shared, R, axis=1)
    values = (own + coefs[None, :] * shared_cols) * FF ** (-0.5)
    return values.astype(jnp.bfloat16)


def touch_ends(drawn, stream_key, smallest, high):
    longest = drawn.shape.index(max(drawn.shape))
    spots = []
    for shift in (0, 1):
        where = [jax.random.randint(jax.random.fold_in(stream_key, axis), (), 0, length) for axis, length in enumerate(drawn.shape)]
        where[longest] = (where[longest] + shift) % drawn.shape[longest]
        spots.append(tuple(where))
    return drawn.at[spots[0]].set(smallest).at[spots[1]].set(high)


def raised(entries, own_key, source, target, parts, factor):
    owner, partner = [(jnp.arange(entries.shape[axis_at]) // (entries.shape[axis_at] // parts)).reshape([-1 if axis == axis_at else 1 for axis in range(entries.ndim)]) for axis_at in (source, target)]
    chosen = jax.random.permutation(own_key, parts)[partner]
    strong = (owner == chosen) | (owner == (partner + parts // 2) % parts)
    return jnp.where(strong, factor * entries, entries)


def steps_of(key, dims, shards, low, high):
    def one(dim, shards_of):
        draws = jax.random.uniform(jax.random.fold_in(jax.random.fold_in(key, 6), dim), (shards_of,), jnp.float32, low / len(shards), high / len(shards))
        return jnp.repeat(jnp.exp(draws), dims[dim] // shards_of).reshape((-1,) + (1,) * (len(dims) - dim - 1))

    loudness = one(*shards[0])
    for cut in shards[1:]:
        loudness = loudness * one(*cut)
    return loudness


def gaussian(rng, dims, width, reach, cuts=(), held_as=jnp.bfloat16):
    level = steps_of(rng, dims, cuts, -0.22, 0.18) if cuts else 1.0
    result = jax.random.normal(rng, dims, jnp.float32) * width * level
    return jnp.minimum(jnp.maximum(result, -reach), reach).astype(held_as)


def noise_with(own_key, shape, deviation, most, cuts, heavy, held_as=jnp.bfloat16):
    result = deviation * jax.random.normal(own_key, shape, jnp.float32)
    if cuts:
        result = result * steps_of(own_key, shape, cuts, -0.22, 0.18)
    return jnp.clip(raised(result, jax.random.fold_in(own_key, 3), *heavy), -most, most).astype(held_as)


def setup_inputs(seed: int = 0) -> dict:
    key_list = jax.random.split(jax.random.key(seed), 8)
    return {
        "hidden": gaussian(key_list[0], (TOKENS, FF), 1.0, 6.0, ((0, 32), (1, 16))),
        "tenant_ids": touch_ends(jax.random.randint(key_list[1], (BLOCKS,), 0, K), jax.random.fold_in(key_list[1], 1), 0, K - 1).astype(jnp.int32),
        "base_weight": noise_with(key_list[2], (FF, D), FF ** -0.5, 0.09375, ((0, 16), (1, 32)), (0, 1, 32, 2.75)),
        "adapter_in": draw_adapter_in(jax.random.fold_in(key_list[7], 71), 0),
        "adapter_out": gaussian(key_list[4], (ADAPT, D), (4 * R) ** -0.5, 0.5, ((1, 16),)),
        "magnitude": jnp.clip(jnp.exp(math.log(2.0) - 1.3862944 * jax.random.uniform(key_list[5], (K, D), jnp.float32) ** steps_of(key_list[5], (K, D), ((1, 16),), -0.2, 0.2)), 0.5, 2.0),
        "cotangent": gaussian(key_list[6], (TOKENS, D), 1.0, 6.0, ((0, 32), (1, 16))),
    }


def reference(hidden, tenant_ids, base_weight, adapter_in, adapter_out, magnitude, cotangent):
    highest = lax.Precision.HIGHEST
    tenant = tenant_ids[(jnp.arange(TOKENS, dtype=jnp.int32) // BLOCK).astype(jnp.int32)]
    col_owner = jnp.arange(K * R, dtype=jnp.int32) // R
    col_mask = (tenant[:, None] == col_owner[None, :]).astype(jnp.float32)
    onehot = (tenant[:, None] == jnp.arange(K, dtype=jnp.int32)[None, :]).astype(jnp.float32)
    lowrank = jnp.dot(hidden, adapter_in, preferred_element_type=jnp.float32) * col_mask
    out_wide = adapter_out.astype(jnp.float32)
    summed = jnp.dot(hidden, base_weight, preferred_element_type=jnp.float32) + jnp.dot(lowrank, out_wide, precision=highest)
    column_sq = lax.optimization_barrier(jnp.sum(jnp.square(base_weight.astype(jnp.float32)), axis=0))
    cross_term = jnp.dot(adapter_in.T, base_weight, preferred_element_type=jnp.float32)
    block_mask = (col_owner[:, None] == col_owner[None, :]).astype(jnp.float32)
    adapter_gram = jnp.dot(adapter_in.T, adapter_in, preferred_element_type=jnp.float32) * block_mask
    inner_term = jnp.dot(adapter_gram, out_wide, precision=highest)
    per_tenant = ((2.0 * cross_term + inner_term) * out_wide).reshape(K, R, D).sum(axis=1)
    squares = column_sq[None, :] + per_tenant
    length = jnp.sqrt(squares + 1e-06)
    col_scale = magnitude / length
    tok_scale = jnp.dot(onehot, col_scale, precision=highest)
    adapted = (summed * tok_scale).astype(jnp.bfloat16)
    slopes = (cotangent.astype(jnp.float32) * tok_scale).astype(jnp.bfloat16)
    back_adapt = jnp.dot(slopes, adapter_out.T, preferred_element_type=jnp.float32) * col_mask
    input_grad = (jnp.dot(slopes, base_weight.T, preferred_element_type=jnp.float32) + jnp.dot(back_adapt, adapter_in.astype(jnp.float32).T, precision=highest)).astype(jnp.bfloat16)
    grad_in = jnp.dot(hidden.astype(jnp.float32).T, back_adapt, precision=highest)
    grad_out = jnp.dot(lowrank.T, slopes.astype(jnp.float32), precision=highest)
    grad_mag = jnp.dot(onehot.T, cotangent.astype(jnp.float32) * summed, precision=highest) / length
    return (adapted, input_grad, grad_in, grad_out, grad_mag)
```

```python
import functools

import jax
import jax.numpy as jnp
from jax import lax
from jax.experimental import pallas as pl
from jax.experimental.pallas import tpu as pltpu
from jax.sharding import PartitionSpec as P

epsilon = 1e-06
f32 = jnp.float32
bf16 = jnp.bfloat16
MESH = pl.DeviceIdType.MESH


def dot(lhs, rhs, lhs_dim, rhs_dim, precision=None):
    return lax.dot_general(
        lhs,
        rhs,
        (((lhs_dim,), (rhs_dim,)), ((), ())),
        precision=precision,
        preferred_element_type=f32,
    )


def loop(count, body):
    lax.fori_loop(0, count, lambda i, c: (body(i), c)[1], 0)


def kernel(
    h, tid, w, a, o, mag, cot,
    adapted, ig, gin, gout, gmag,
    wbuf, hbuf, obuf, lrs, lrr, lrb, sqs, sqr, sqb, sqf, slb, gbuf, cst, crecv,
    igacc, igs, igr, gpart, grecv, gx, gxr, gres, gms, gmr, gmx, gmxr,
    ring_send, ring_right, ring_left, h_send, h_recv, o_send, o_recv, lr_send, lr_recv,
    s1_send, s1_recv, s2_send, s2_recv, g_send, g_recv, f_send, c_send, c_recv,
    ig_send, ig_recv, rs_send, rs_recv, gx_send, gx_recv, ag_send, ag_recv,
    gm_send, gm_recv, gmx_send, gmx_recv,
    *, nt, nz,
):
    tok, ffl = h.shape
    adapt = a.shape[1]
    tenants = mag.shape[0]
    rank = adapt // tenants
    nm = nt // 2
    far = nz // 2
    half_rows = ffl // 2
    d = lax.axis_index("dp")
    t = lax.axis_index("tensor")
    yl = d // nz
    z = d % nz
    core = t % 2
    pair = (1 - yl) * nz + z
    mine = t % nm
    plane = t // nm
    in_plane = plane == yl

    def remote(src, dst, send, recv, dp, tensor):
        return pltpu.make_async_remote_copy(
            src_ref=src, dst_ref=dst, send_sem=send, recv_sem=recv,
            device_id=(dp, tensor), device_id_type=MESH,
        )

    def wait_in(ref, sem):
        pltpu.make_async_copy(ref, ref, sem).wait()

    wait_out = wait_in

    barrier = pltpu.get_barrier_semaphore()

    def greet_plane(i):
        s = i // nt
        u = i % nt

        @pl.when((s != yl) | (u != t))
        def _():
            pl.semaphore_signal(barrier, inc=1, device_id=(s * nz + z, u), device_id_type=MESH)

    def greet_column(i):
        @pl.when(i % nz != z)
        def _():
            pl.semaphore_signal(barrier, inc=1, device_id=(i, t), device_id_type=MESH)

    loop(2 * nt, greet_plane)
    loop(2 * nz, greet_column)
    pl.semaphore_wait(barrier, 2 * nt - 1 + 2 * (nz - 1))

    def ring(src, slot, half, step, right):
        rows = pl.ds(half * half_rows, half_rows)
        src = src.at[rows] if src is w else src.at[slot, rows]
        to = (z + (1 if right else nz - 1)) % nz
        sems = ring_right if right else ring_left
        return remote(
            src, wbuf.at[slot, rows], ring_send, sems.at[(step - 1) * 2 + half], yl * nz + to, t
        )

    def carried(step, half, right):
        return step < far or half == (0 if right else 1)

    def ring_step(step):
        for half in (0, 1):
            for right in (True, False):
                if not carried(step, half, right):
                    continue
                slot = (z + (nz - step if right else step)) % nz
                ring(wbuf, slot, half, step, right).wait_recv()
                if step < far and carried(step + 1, half, right):
                    ring(wbuf, slot, half, step + 1, right).start()

    for half in (0, 1):
        for right in (True, False):
            if carried(1, half, right):
                ring(w, z, half, 1, right).start()

    @pl.when(in_plane)
    def _():
        def send(u):
            @pl.when(u != t)
            def _():
                remote(o, obuf.at[mine], o_send, o_recv, d, u).start()

        loop(nt, send)
        obuf[mine] = o[...]

    remote(h, hbuf.at[yl], h_send, h_recv, pair, t).start()

    owner = lax.div(lax.broadcasted_iota(jnp.int32, (tok, adapt), 1), rank)
    row_owner = lax.div(lax.broadcasted_iota(jnp.int32, (adapt, tok), 0), rank)
    tenant = tid[d // 2]

    lr = jnp.where(owner == tenant, dot(h[...], a[...], 1, 0), 0.0)
    lrb[yl] = lr.astype(bf16)
    turned = lr.T
    packed = turned[0:rank]
    for k in range(1, tenants):
        packed = packed + turned[k * rank:(k + 1) * rank]
    lrs[...] = packed.astype(bf16)

    def send_lr(u):
        @pl.when(u != t)
        def _():
            remote(lrs, lrr.at[t], lr_send, lr_recv, d, u).start()

    loop(nt, send_lr)
    lrr[t] = lrs[...]
    wbuf[z] = w[...]
    hbuf[yl] = h[...]
    grow = lax.div(lax.broadcasted_iota(jnp.int32, (adapt, adapt), 0), rank)
    gcol = lax.div(lax.broadcasted_iota(jnp.int32, (adapt, adapt), 1), rank)
    gram = jnp.where(grow == gcol, dot(a[...], a[...], 0, 0), 0.0)
    cross = dot(a[...], w[...], 0, 0)
    wide = w[...].astype(f32)
    column_sq = jnp.sum(wide * wide, axis=0, keepdims=True)

    ring_step(1)

    @pl.when(in_plane)
    def _():
        wait_in(obuf.at[pl.ds(0, nm - 1)], o_recv)

    @pl.when(jnp.logical_not(in_plane))
    def _():
        wait_in(obuf.at[pl.ds(0, nm)], o_recv)

    own = obuf[z // 2, :, pl.ds(pl.multiple_of((z % 2) * 128, 128), 128)].astype(f32)
    inner = dot(gram, own, 1, 0, lax.Precision.HIGHEST)
    prod = (2.0 * cross + inner) * own
    rows = [
        jnp.sum(prod[k * rank:(k + 1) * rank], axis=0, keepdims=True) + column_sq
        for k in range(tenants)
    ]
    sqs[...] = jnp.concatenate(rows + [jnp.zeros((8 - tenants, 128), f32)], axis=0)
    lead = d // 2

    @pl.when(t != lead)
    def _():
        remote(sqs, sqr.at[t], s1_send, s1_recv, d, lead).start()

    @pl.when(t == lead)
    def _():
        sqr[t] = sqs[...]

    if far > 2:
        ring_step(2)

    @pl.when(t == lead)
    def _():
        wait_in(sqr.at[pl.ds(0, nt - 1)], s1_recv)
        total = sqr[0]
        for u in range(1, nt):
            total = total + sqr[u]
        sqb[...] = total

        def send(i):
            @pl.when(i != d)
            def _():
                remote(sqb, sqf.at[d % 2], s2_send, s2_recv.at[d % 2], i, t).start()

        loop(2 * nz, send)
        sqf[d % 2] = total

    if far > 3:
        ring_step(3)

    for e in (0, 1):
        @pl.when(d != 2 * t + e)
        def _(e=e):
            wait_in(sqf.at[e], s2_recv.at[e])

    squares = jnp.concatenate([sqf[0], sqf[1]], axis=1)[0:tenants]
    length = jnp.sqrt(squares + epsilon)
    col_scale = mag[...] / length
    one_hot = lax.broadcasted_iota(jnp.int32, (tenants, 256), 0) == tenant
    scale = jnp.sum(jnp.where(one_hot, col_scale, 0.0), axis=0, keepdims=True)
    slb[...] = (cot[...].astype(f32) * scale).astype(bf16)
    slot = mine * 2 + yl

    def send_slopes(q):
        u = 2 * q + core

        @pl.when(jnp.logical_not(in_plane) | (u != t))
        def _():
            remote(slb, gbuf.at[slot], g_send, g_recv.at[slot], plane * nz + z, u).start()

    loop(nt // 2, send_slopes)

    @pl.when(in_plane)
    def _():
        gbuf[slot] = slb[...]

    if far > 4:
        ring_step(4)

    wait_in(hbuf.at[1 - yl], h_recv)
    other = dot(hbuf[1 - yl], a[...], 1, 0)
    lrb[1 - yl] = jnp.where(owner == tid[pair // 2], other, 0.0).astype(bf16)

    def share(b):
        m = b // 2
        cols = pl.ds(pl.multiple_of((b % 2) * 128, 128), 128)
        for s in (0, 1):
            part = dot(hbuf[s], wbuf[b], 1, 0) + dot(lrb[s], obuf[m, :, cols], 1, 0)
            cst[b * 2 + s] = part.astype(bf16)
            here = (s == yl) & in_plane & (m == mine)

            @pl.when(here)
            def _():
                crecv[t * 2 + b % 2] = cst[b * 2 + s]

            @pl.when(jnp.logical_not(here))
            def _():
                remote(
                    cst.at[b * 2 + s], crecv.at[t * 2 + b % 2], c_send, c_recv,
                    s * nz + z, yl * nm + m,
                ).start()

    ready = min(4, far - 1)
    loop(2 * ready + 1, lambda i: share((z + nz - ready + i) % nz))

    def relay(i):
        at = (2 * (i // 2) + core) * 2 + i % 2

        @pl.when(jnp.logical_not(in_plane) | (at != slot))
        def _():
            wait_in(gbuf.at[at], g_recv.at[at])

        remote(gbuf.at[at], gbuf.at[at], f_send, g_recv.at[at], d, t + 1 - 2 * core).start()

    for step in range(ready + 1, far):
        ring_step(step)
        loop(2, lambda i: share((z + step + i * (2 * nz - 2 * step)) % nz))
    loop(nm, relay)

    def received(i):
        at = (2 * (i // 2) + 1 - core) * 2 + i % 2
        wait_in(gbuf.at[at], g_recv.at[at])

    loop(nm, received)

    def slopes_of(m):
        return jnp.concatenate([gbuf[2 * m], gbuf[2 * m + 1]], axis=0)

    back = dot(slopes_of(0), obuf[0], 1, 1)
    for m in range(1, nm):
        back = back + dot(slopes_of(m), obuf[m], 1, 1)
    tenant_col = jnp.concatenate(
        [jnp.full((tok, adapt), tid[(s * nz + z) // 2], jnp.int32) for s in (0, 1)], axis=0
    )
    owner2 = lax.div(lax.broadcasted_iota(jnp.int32, (2 * tok, adapt), 1), rank)
    back = jnp.where(owner2 == tenant_col, back, 0.0).astype(bf16)

    hidden2 = jnp.concatenate([hbuf[0], hbuf[1]], axis=0)
    grad_in = dot(hidden2, back, 0, 0)
    wait_in(lrr.at[pl.ds(0, nt - 1)], lr_recv)
    low = lrr[0].astype(f32)
    for u in range(1, nt):
        low = low + lrr[u].astype(f32)
    low = jnp.where(row_owner == tenant, jnp.concatenate([low] * tenants, axis=0), 0.0)
    high = low.astype(bf16)
    rest = (low - high.astype(f32)).astype(bf16)
    grad_out = dot(high, slb[...], 1, 0) + dot(rest, slb[...], 1, 0)
    grad_out = jnp.concatenate([grad_out[:, 0:128], grad_out[:, 128:256]], axis=0)
    in_rows = ffl // nz
    out_rows = 2 * adapt // nz
    pad = gpart.shape[1] - in_rows - out_rows
    for i in range(nz):
        parts = [
            grad_out[i * out_rows:(i + 1) * out_rows],
            grad_in[i * in_rows:(i + 1) * in_rows],
        ]
        if pad:
            parts.append(jnp.zeros((pad, 128), f32))
        gpart[i] = jnp.concatenate(parts, axis=0).astype(bf16)
    grecv[z] = gpart[z]

    def scatter(i):
        @pl.when(i != z)
        def _():
            remote(gpart.at[i], grecv.at[z], rs_send, rs_recv, yl * nz + i, t).start()

    loop(nz, scatter)

    last = ((z + far) % nz) // 2

    def backward(m):
        weight = jnp.concatenate([wbuf[2 * m], wbuf[2 * m + 1]], axis=1)
        for s in (0, 1):
            igacc[s] += dot(gbuf[2 * m + s], weight, 1, 1)

    for s in (0, 1):
        igacc[s] = dot(back[s * tok:(s + 1) * tok], a[...], 1, 1)
    loop(nm - 1, lambda i: backward((last + 1 + i) % nm))

    ring_step(far)
    share((z + far) % nz)
    backward(last)
    igs[...] = igacc[1 - yl].astype(bf16)
    remote(igs, igr, ig_send, ig_recv, pair, t).start()

    @pl.when(in_plane)
    def _():
        wait_in(crecv.at[pl.ds(0, 2 * nt - 2)], c_recv)

    @pl.when(jnp.logical_not(in_plane))
    def _():
        wait_in(crecv, c_recv)

    sums = []
    for half in (0, 1):
        cols = slice(half * 128, (half + 1) * 128)
        total = crecv[half].astype(f32)
        for u in range(1, nt):
            total = total + crecv[2 * u + half].astype(f32)
        adapted[:, cols] = (total * scale[:, cols]).astype(bf16)
        sums.append(jnp.sum(cot[:, cols].astype(f32) * total, axis=0, keepdims=True))
    hot = lax.broadcasted_iota(jnp.int32, (tenants, 128), 0) == tenant
    gms[...] = jnp.concatenate([jnp.where(hot, part, 0.0) for part in sums], axis=0)
    gmr[z] = gms[...]

    def send_mag(i):
        @pl.when(i != z)
        def _():
            remote(gms, gmr.at[z], gm_send, gm_recv, yl * nz + i, t).start()

    loop(nz, send_mag)

    wait_in(grecv.at[pl.ds(0, nz - 1)], rs_recv)
    total = grecv[0].astype(f32)
    for i in range(1, nz):
        total = total + grecv[i].astype(f32)
    gx[...] = total
    remote(gx, gxr, gx_send, gx_recv, pair, t).start()

    wait_in(igr, ig_recv)
    ig[...] = (igacc[yl] + igr[...].astype(f32)).astype(bf16)

    wait_in(gxr, gx_recv)
    gres[z] = (gx[...] + gxr[...]).astype(bf16)

    def spread(i):
        @pl.when(i != z)
        def _():
            remote(gres.at[z], gres.at[z], ag_send, ag_recv, yl * nz + i, t).start()

    loop(nz, spread)

    wait_in(gmr.at[pl.ds(0, nz - 1)], gm_recv)
    total = gmr[0]
    for i in range(1, nz):
        total = total + gmr[i]
    gmx[...] = total
    remote(gmx, gmxr, gmx_send, gmx_recv, pair, t).start()
    wait_in(gmxr, gmx_recv)
    total = gmx[...] + gmxr[...]
    gmag[...] = jnp.concatenate([total[0:tenants], total[tenants:]], axis=1) / length

    wait_in(gres.at[pl.ds(0, nz - 1)], ag_recv)
    for i in range(nz):
        part = gres[i].astype(f32)
        half, row = divmod(i * out_rows, adapt)
        gout[row:row + out_rows, half * 128:(half + 1) * 128] = part[0:out_rows]
        gin[i * in_rows:(i + 1) * in_rows] = part[out_rows:out_rows + in_rows]

    wait_out(wbuf.at[pl.ds(0, nz - 1)], ring_send)
    wait_out(hbuf.at[0], h_send)

    @pl.when(in_plane)
    def _():
        wait_out(obuf.at[pl.ds(0, nt - 1)], o_send)
        wait_out(gbuf.at[pl.ds(0, nt // 2 - 1)], g_send)
        wait_out(cst.at[pl.ds(0, 2 * nz - 2)], c_send)

    @pl.when(jnp.logical_not(in_plane))
    def _():
        wait_out(gbuf.at[pl.ds(0, nt // 2)], g_send)
        wait_out(cst, c_send)

    wait_out(lrr.at[pl.ds(0, nt - 1)], lr_send)

    @pl.when(t != lead)
    def _():
        wait_out(sqs, s1_send)

    @pl.when(t == lead)
    def _():
        wait_out(sqr.at[pl.ds(0, 2 * nz - 1)], s2_send)

    wait_out(gbuf.at[pl.ds(0, nm)], f_send)
    wait_out(igs, ig_send)
    wait_out(gpart.at[pl.ds(0, nz - 1)], rs_send)
    wait_out(gx, gx_send)
    wait_out(gres.at[pl.ds(0, nz - 1)], ag_send)
    wait_out(gmr.at[pl.ds(0, nz - 1)], gm_send)
    wait_out(gmx, gmx_send)


def per_device(nt, nz, hidden, tenant_ids, base_weight, adapter_in, adapter_out, magnitude, cotangent):
    tok, ffl = hidden.shape
    adapt = adapter_in.shape[1]
    nm = nt // 2
    grad_rows = -(-(ffl // nz + 2 * adapt // nz) // 16) * 16
    vmem = pl.BlockSpec(memory_space=pltpu.VMEM)
    dma = pltpu.SemaphoreType.DMA
    tile = (8, 128)
    scratch = [
        pltpu.VMEM((nz, ffl, 128), bf16),
        pltpu.VMEM((2, tok, ffl), bf16),
        pltpu.VMEM((nt, adapt, 256), bf16),
        pltpu.VMEM((adapt // 4, tok), bf16),
        pltpu.VMEM((nt, adapt // 4, tok), bf16),
        pltpu.VMEM((2, tok, adapt), bf16),
        pltpu.VMEM(tile, f32),
        pltpu.VMEM((2 * nz,) + tile, f32),
        pltpu.VMEM(tile, f32),
        pltpu.VMEM((2,) + tile, f32),
        pltpu.VMEM((tok, 256), bf16),
        pltpu.VMEM((nt, tok, 256), bf16),
        pltpu.VMEM((2 * nz, tok, 128), bf16),
        pltpu.VMEM((2 * nt, tok, 128), bf16),
        pltpu.VMEM((2, tok, ffl), f32),
        pltpu.VMEM((tok, ffl), bf16),
        pltpu.VMEM((tok, ffl), bf16),
        pltpu.VMEM((nz, grad_rows, 128), bf16),
        pltpu.VMEM((nz, grad_rows, 128), bf16),
        pltpu.VMEM((grad_rows, 128), f32),
        pltpu.VMEM((grad_rows, 128), f32),
        pltpu.VMEM((nz, grad_rows, 128), bf16),
        pltpu.VMEM(tile, f32),
        pltpu.VMEM((nz,) + tile, f32),
        pltpu.VMEM(tile, f32),
        pltpu.VMEM(tile, f32),
        dma, dma((nz,)), dma((nz,)), dma, dma, dma, dma, dma, dma,
        dma, dma, dma, dma((2,)), dma, dma((nt,)), dma, dma, dma,
        dma, dma, dma, dma, dma, dma, dma, dma,
        dma, dma, dma, dma,
    ]
    return pl.pallas_call(
        functools.partial(kernel, nt=nt, nz=nz),
        out_shape=(
            jax.ShapeDtypeStruct((tok, 256), bf16),
            jax.ShapeDtypeStruct((tok, ffl), bf16),
            jax.ShapeDtypeStruct((ffl, adapt), f32),
            jax.ShapeDtypeStruct((adapt, 256), f32),
            jax.ShapeDtypeStruct(magnitude.shape, f32),
        ),
        in_specs=[vmem, pl.BlockSpec(memory_space=pltpu.SMEM)] + [vmem] * 5,
        out_specs=[vmem] * 5,
        scratch_shapes=scratch,
        compiler_params=pltpu.CompilerParams(
            collective_id=0, has_side_effects=True, vmem_limit_bytes=48 * 2**20
        ),
        name="dora",
    )(hidden, tenant_ids, base_weight, adapter_in, adapter_out, magnitude, cotangent)


def solution(mesh):
    nt = mesh.shape["tensor"]
    nz = mesh.shape["dp"] // 2
    return jax.shard_map(
        functools.partial(per_device, nt, nz),
        mesh=mesh,
        in_specs=(
            P("dp", "tensor"),
            P(),
            P("tensor", "dp"),
            P("tensor", None),
            P(None, "tensor"),
            P(None, "tensor"),
            P("dp", "tensor"),
        ),
        out_specs=(
            P("dp", "tensor"),
            P("dp", "tensor"),
            P("tensor", None),
            P(None, "tensor"),
            P(None, "tensor"),
        ),
        check_vma=False,
    )
```

```python
import functools

import jax
import jax.numpy as jnp
from jax import lax
from jax.experimental import pallas as pl
from jax.experimental.pallas import tpu as pltpu
from jax.sharding import PartitionSpec as P

epsilon = 1e-06
f32 = jnp.float32
bf16 = jnp.bfloat16
MESH = pl.DeviceIdType.MESH


def dot(lhs, rhs, lhs_dim, rhs_dim, precision=None):
    return lax.dot_general(
        lhs,
        rhs,
        (((lhs_dim,), (rhs_dim,)), ((), ())),
        precision=precision,
        preferred_element_type=f32,
    )


def loop(count, body):
    lax.fori_loop(0, count, lambda i, c: (body(i), c)[1], 0)


def kernel(
    h_hbm, tid, w_hbm, a_hbm, o_hbm, mag_hbm, cot_hbm,
    adapted, ig, gin, gout, gmag,
    a, o, mag, cot, wbuf, hbuf, ob, obd, lrs, lrr, bas, bar, sqs, sqr, sqb, sqf, slb, gbuf,
    cacc, sst, srecv, cst, crecv, igacc, igs, igr, gpart, grecv, gx, gxr, gres, gt,
    gms, gmr, gmx, gmxr,
    in_sem, ring_send, ring_right, ring_left, h_send, h_recv, o_send, o_recv,
    lr_send, lr_recv, ba_send, ba_recv, s1_send, s1_recv, s2_send, s2_recv,
    g_send, g_recv, f_send, sib_send, sib_recv, c_send, c_recv, ig_send, ig_recv,
    rs_send, rs_recv, gx_send, gx_recv, ag_send, ag_recv, gm_send, gm_recv, gmx_send, gmx_recv,
    *, nt, nz,
):
    tok, ffl = igs.shape
    adapt = a.shape[1]
    tenants = mag.shape[0]
    rank = adapt // tenants
    nm = nt // 2
    far = nz // 2
    half_rows = ffl // 2
    d = lax.axis_index("dp")
    t = lax.axis_index("tensor")
    yl = d // nz
    z = d % nz
    core = t % 2
    pair = (1 - yl) * nz + z
    sibling = t + 1 - 2 * core
    mine = t % nm
    plane = t // nm
    in_plane = plane == yl

    def remote(src, dst, send, recv, dp, tensor):
        return pltpu.make_async_remote_copy(
            src_ref=src, dst_ref=dst, send_sem=send, recv_sem=recv,
            device_id=(dp, tensor), device_id_type=MESH,
        )

    def wait_in(ref, sem):
        pltpu.make_async_copy(ref, ref, sem).wait()

    wait_out = wait_in

    loads = [
        pltpu.make_async_copy(src, dst, in_sem.at[i])
        for i, (src, dst) in enumerate((
            (w_hbm, wbuf.at[z]), (h_hbm, hbuf.at[yl]), (a_hbm, a), (o_hbm, o),
            (mag_hbm, mag), (cot_hbm, cot),
        ))
    ]
    for load in loads:
        load.start()

    barrier = pltpu.get_barrier_semaphore()

    def greet_plane(i):
        s = i // nt
        u = i % nt

        @pl.when((s != yl) | (u != t))
        def _():
            pl.semaphore_signal(barrier, inc=1, device_id=(s * nz + z, u), device_id_type=MESH)

    def greet_column(i):
        @pl.when(i % nz != z)
        def _():
            pl.semaphore_signal(barrier, inc=1, device_id=(i, t), device_id_type=MESH)

    loop(2 * nt, greet_plane)
    loop(2 * nz, greet_column)
    for load in loads:
        load.wait()
    pl.semaphore_wait(barrier, 2 * nt - 1 + 2 * (nz - 1))

    def ring(slot, half, step, right):
        rows = pl.ds(half * half_rows, half_rows)
        to = (z + (1 if right else nz - 1)) % nz
        sems = ring_right if right else ring_left
        ref = wbuf.at[slot, rows]
        return remote(ref, ref, ring_send, sems.at[(step - 1) * 2 + half], yl * nz + to, t)

    def carried(step, half, right):
        return step < far or half == (0 if right else 1)

    def ring_step(step):
        for half in (0, 1):
            for right in (True, False):
                if not carried(step, half, right):
                    continue
                slot = (z + (nz - step if right else step)) % nz
                ring(slot, half, step, right).wait_recv()
                if step < far and carried(step + 1, half, right):
                    ring(slot, half, step + 1, right).start()

    for half in (0, 1):
        for right in (True, False):
            if carried(1, half, right):
                ring(z, half, 1, right).start()

    lead = d // 2
    ocols = pl.ds(pl.multiple_of((z % 2) * 128, 128), 128)

    @pl.when(t == lead)
    def _():
        ob[...] = o[:, ocols]

        def send(u):
            @pl.when(u != t)
            def _():
                remote(ob, ob, o_send, o_recv, d, u).start()

        loop(nt, send)

    remote(hbuf.at[yl], hbuf.at[yl], h_send, h_recv, pair, t).start()

    tenant = tid[d // 2]

    owner = lax.div(lax.broadcasted_iota(jnp.int32, (tok, adapt), 1), rank)
    turned = jnp.where(owner == tenant, dot(hbuf[yl], a[...], 1, 0), 0.0).T
    packed = turned[0:rank]
    for k in range(1, tenants):
        packed = packed + turned[k * rank:(k + 1) * rank]
    lrs[...] = packed.astype(bf16)

    def send_lr(u):
        @pl.when(u != t)
        def _():
            remote(lrs, lrr.at[t], lr_send, lr_recv, d, u).start()

    loop(nt, send_lr)
    lrr[t] = lrs[...]
    grow = lax.div(lax.broadcasted_iota(jnp.int32, (adapt, adapt), 0), rank)
    gcol = lax.div(lax.broadcasted_iota(jnp.int32, (adapt, adapt), 1), rank)
    gram = jnp.where(grow == gcol, dot(a[...], a[...], 0, 0), 0.0)
    cross = dot(a[...], wbuf[z], 0, 0)
    wide = wbuf[z].astype(f32)
    column_sq = jnp.sum(wide * wide, axis=0, keepdims=True)

    ring_step(1)

    @pl.when(t != lead)
    def _():
        wait_in(ob, o_recv)

    own = ob[...].astype(f32)
    inner = dot(gram, own, 1, 0, lax.Precision.HIGHEST)
    prod = (2.0 * cross + inner) * own
    rows = [
        jnp.sum(prod[k * rank:(k + 1) * rank], axis=0, keepdims=True) + column_sq
        for k in range(tenants)
    ]
    sqs[...] = jnp.concatenate(rows + [jnp.zeros((8 - tenants, 128), f32)], axis=0)

    @pl.when(t != lead)
    def _():
        remote(sqs, sqr.at[t], s1_send, s1_recv, d, lead).start()

    @pl.when(t == lead)
    def _():
        sqr[t] = sqs[...]

    if far > 2:
        ring_step(2)

    @pl.when(t == lead)
    def _():
        wait_in(sqr.at[pl.ds(0, nt - 1)], s1_recv)
        total = sqr[0]
        for u in range(1, nt):
            total = total + sqr[u]
        sqb[...] = total

        def send(i):
            to = (i % 2) * nz + (z + far + (i // 4) * (1 - (i // 2) % 2 * 2) + nz - (i // 2) % 2) % nz

            @pl.when(to != d)
            def _():
                remote(sqb, sqf.at[d % 2], s2_send, s2_recv.at[d % 2], to, t).start()

        loop(2 * nz, send)
        sqf[d % 2] = total

    def share(b):
        sst[b] = dot(hbuf[1 - core], wbuf[b], 1, 0).astype(bf16)
        remote(sst.at[b], srecv.at[b], sib_send, sib_recv.at[b], d, sibling).start()
        cacc[b] = dot(hbuf[core], wbuf[b], 1, 0)

    def deliver(b):
        m = b // 2
        place = (t // 2) * 2 + b % 2
        wait_in(srecv.at[b], sib_recv.at[b])
        cst[b] = (cacc[b] + srecv[b].astype(f32)).astype(bf16)
        here = (core == yl) & in_plane & (m == mine)

        @pl.when(here)
        def _():
            crecv[place] = cst[b]

        @pl.when(jnp.logical_not(here))
        def _():
            remote(
                cst.at[b], crecv.at[place], c_send, c_recv, core * nz + z, yl * nm + m
            ).start()

    def near(step):
        return 2 * step + 1, lambda i: (z + nz - step + i) % nz

    def at(step):
        return 2, lambda i: (z + step + i * (2 * nz - 2 * step)) % nz

    def each(blocks, body):
        loop(blocks[0], lambda i: body(blocks[1](i)))

    ready = min(3, far - 1)
    if far > 3:
        ring_step(3)
    wait_in(hbuf.at[1 - yl], h_recv)
    each(near(ready), share)
    if far > 4:
        ring_step(4)

    for e in (0, 1):
        @pl.when(d != 2 * t + e)
        def _(e=e):
            wait_in(sqf.at[e], s2_recv.at[e])

    squares = jnp.concatenate([sqf[0], sqf[1]], axis=1)[0:tenants]
    length = jnp.sqrt(squares + epsilon)
    col_scale = mag[...] / length
    one_hot = lax.broadcasted_iota(jnp.int32, (tenants, 256), 0) == tenant
    scale = jnp.sum(jnp.where(one_hot, col_scale, 0.0), axis=0, keepdims=True)
    slb[...] = (cot[...].astype(f32) * scale).astype(bf16)
    slot = mine * 2 + yl

    def send_slopes(q):
        u = 2 * q + core

        @pl.when(jnp.logical_not(in_plane) | (u != t))
        def _():
            remote(slb, gbuf.at[slot], g_send, g_recv.at[slot], plane * nz + z, u).start()

    loop(nt // 2, send_slopes)

    @pl.when(in_plane)
    def _():
        gbuf[slot] = slb[...]

    out_ten = jnp.zeros((rank, 256), f32)
    for k in range(tenants):
        out_ten = jnp.where(tenant == k, o[k * rank:(k + 1) * rank].astype(f32), out_ten)
    out_ten = out_ten.astype(bf16)
    bas[...] = dot(out_ten, slb[...], 1, 1).astype(bf16)

    def send_back(u):
        @pl.when(u != t)
        def _():
            remote(bas, bar.at[t], ba_send, ba_recv, d, u).start()

    loop(nt, send_back)
    bar[t] = bas[...]

    if far > 5:
        ring_step(5)
    each(near(ready), deliver)
    for step in range(ready + 1, min(far, 6)):
        each(at(step), share)
    if far > 6:
        ring_step(6)
        for step in range(ready + 1, 6):
            each(at(step), deliver)
        each(at(6), share)

    wait_in(bar.at[pl.ds(0, nt - 1)], ba_recv)
    back = bar[0].astype(f32)
    for u in range(1, nt):
        back = back + bar[u].astype(f32)
    wait_in(lrr.at[pl.ds(0, nt - 1)], lr_recv)
    low = lrr[0].astype(f32)
    for u in range(1, nt):
        low = low + lrr[u].astype(f32)
    low_high = low.astype(bf16)
    low_rest = (low - low_high.astype(f32)).astype(bf16)
    back_high = back.astype(bf16)
    back_rest = (back - back_high.astype(f32)).astype(bf16)
    grads = [
        dot(back_high, hbuf[yl], 1, 0) + dot(back_rest, hbuf[yl], 1, 0),
        dot(low_high, slb[...], 1, 0) + dot(low_rest, slb[...], 1, 0),
    ]
    tiles = []
    for grad in grads:
        for j in range(grad.shape[1] // 128):
            for g in range(rank // 8):
                tiles.append(grad[g * 8:(g + 1) * 8, j * 128:(j + 1) * 128])
    per = gx.shape[0] // (8 * tenants)
    owners = len(tiles) // per
    for i in range(owners):
        parts = tiles[i * per:(i + 1) * per]
        parts.append(jnp.zeros((gpart.shape[1] - 8 * per, 128), f32))
        gpart[i] = jnp.concatenate(parts, axis=0).astype(bf16)

    def scatter(i):
        @pl.when(i != z)
        def _():
            remote(gpart.at[i], grecv.at[z], rs_send, rs_recv, yl * nz + i, t).start()

    loop(owners, scatter)

    @pl.when(z < owners)
    def _():
        grecv[z] = gpart[z]

    if far > 7:
        ring_step(7)
        each(at(6), deliver)
        each(at(7), share)

    row_owner = lax.div(lax.broadcasted_iota(jnp.int32, (adapt, tok), 0), rank)
    full = jnp.where(row_owner == tenant, jnp.concatenate([back] * tenants, axis=0), 0.0)
    igacc[yl] = dot(full.T.astype(bf16), a[...], 1, 1)
    igacc[1 - yl] = jnp.zeros((tok, ffl), f32)
    low_out = dot(low_high, out_ten, 0, 0) + dot(low_rest, out_ten, 0, 0)
    if far > 7:
        each(at(7), deliver)

    ring_step(far)
    share((z + far) % nz)

    def relay(i):
        at = (2 * (i // 2) + core) * 2 + i % 2

        @pl.when(jnp.logical_not(in_plane) | (at != slot))
        def _():
            wait_in(gbuf.at[at], g_recv.at[at])

        remote(gbuf.at[at], gbuf.at[at], f_send, g_recv.at[at], d, sibling).start()

    def received(i):
        at = (2 * (i // 2) + 1 - core) * 2 + i % 2
        wait_in(gbuf.at[at], g_recv.at[at])

    loop(nm, relay)
    deliver((z + far) % nz)
    loop(nm, received)

    def backward(s):
        def body(m):
            weight = jnp.concatenate([wbuf[2 * m], wbuf[2 * m + 1]], axis=1)
            igacc[s] += dot(gbuf[2 * m + s], weight, 1, 1)

        return body

    loop(nm, backward(1 - yl))
    igs[...] = igacc[1 - yl].astype(bf16)
    remote(igs, igr, ig_send, ig_recv, pair, t).start()

    @pl.when(z < owners)
    def _():
        wait_in(grecv.at[pl.ds(0, nz - 1)], rs_recv)
        sums = [jnp.zeros((8 * per, 128), f32)] * tenants
        for i in range(0, nz, 2):
            both = grecv[i].astype(f32) + grecv[i + 1].astype(f32)
            who = tid[(yl * nz + i) // 2]
            sums = [acc + jnp.where(who == k, both[0:8 * per], 0.0) for k, acc in enumerate(sums)]
        gx[...] = jnp.concatenate(sums, axis=0)
        remote(gx, gxr, gx_send, gx_recv, pair, t).start()

    here = in_plane & (core == yl)

    @pl.when(here)
    def _():
        wait_in(crecv.at[pl.ds(0, nt - 2)], c_recv)

    @pl.when(jnp.logical_not(here))
    def _():
        wait_in(crecv, c_recv)

    sums = []
    for half in (0, 1):
        cols = slice(half * 128, (half + 1) * 128)
        total = low_out[:, cols]
        for q in range(nt // 2):
            total = total + crecv[2 * q + half].astype(f32)
        adapted[:, cols] = (total * scale[:, cols]).astype(bf16)
        sums.append(jnp.sum(cot[:, cols].astype(f32) * total, axis=0, keepdims=True))
    hot = lax.broadcasted_iota(jnp.int32, (tenants, 128), 0) == tenant
    gms[...] = jnp.concatenate([jnp.where(hot, part, 0.0) for part in sums], axis=0)

    def send_mag(i):
        to = (z + far + i) % nz

        @pl.when(to != z)
        def _():
            remote(gms, gmr.at[z], gm_send, gm_recv, yl * nz + to, t).start()

    loop(nz, send_mag)
    gmr[z] = gms[...]

    @pl.when(z < owners)
    def _():
        wait_in(gxr, gx_recv)
        gres[z] = (gx[...] + gxr[...]).astype(bf16)

        def spread(i):
            to = (z + far + i) % nz

            @pl.when(to != z)
            def _():
                remote(gres.at[z], gres.at[z], ag_send, ag_recv, yl * nz + to, t).start()

        loop(nz, spread)

    loop(nm, backward(yl))
    wait_in(gmr.at[pl.ds(0, nz - 1)], gm_recv)
    total = gmr[0]
    for i in range(1, nz):
        total = total + gmr[i]
    gmx[...] = total
    remote(gmx, gmxr, gmx_send, gmx_recv, pair, t).start()

    wait_in(igr, ig_recv)
    ig[...] = (igacc[yl] + igr[...].astype(f32)).astype(bf16)

    @pl.when(z < owners)
    def _():
        wait_in(gres.at[pl.ds(0, owners - 1)], ag_recv)

    @pl.when(z >= owners)
    def _():
        wait_in(gres.at[pl.ds(0, owners)], ag_recv)

    for i in range(len(tiles)):
        j, g = divmod(i, rank // 8)
        part = gres[i // per].astype(f32)
        for k in range(tenants):
            row = k * rank + g * 8
            src = (k * per + i % per) * 8
            if j < ffl // 128:
                gt[row:row + 8, j * 128:(j + 1) * 128] = part[src:src + 8]
            else:
                j2 = j - ffl // 128
                gout[row:row + 8, j2 * 128:(j2 + 1) * 128] = part[src:src + 8]
    for j in range(ffl // 128):
        gin[j * 128:(j + 1) * 128] = gt[:, j * 128:(j + 1) * 128].T

    wait_in(gmxr, gmx_recv)
    total = gmx[...] + gmxr[...]
    gmag[...] = jnp.concatenate([total[0:tenants], total[tenants:]], axis=1) / length

    wait_out(wbuf.at[pl.ds(0, nz - 1)], ring_send)
    wait_out(hbuf.at[0], h_send)

    @pl.when(t != lead)
    def _():
        wait_out(sqs, s1_send)

    @pl.when(t == lead)
    def _():
        wait_out(obd.at[pl.ds(0, nt - 1)], o_send)
        wait_out(sqr.at[pl.ds(0, 2 * nz - 1)], s2_send)

    wait_out(lrr.at[pl.ds(0, nt - 1)], lr_send)
    wait_out(bar.at[pl.ds(0, nt - 1)], ba_send)

    @pl.when(in_plane)
    def _():
        wait_out(gbuf.at[pl.ds(0, nt // 2 - 1)], g_send)

    @pl.when(jnp.logical_not(in_plane))
    def _():
        wait_out(gbuf.at[pl.ds(0, nt // 2)], g_send)

    wait_out(gbuf.at[pl.ds(0, nm)], f_send)
    wait_out(sst, sib_send)

    @pl.when(here)
    def _():
        wait_out(cst.at[pl.ds(0, nz - 2)], c_send)

    @pl.when(jnp.logical_not(here))
    def _():
        wait_out(cst, c_send)

    wait_out(igs, ig_send)

    @pl.when(z < owners)
    def _():
        wait_out(gpart.at[pl.ds(0, owners - 1)], rs_send)
        wait_out(gx, gx_send)
        wait_out(gres.at[pl.ds(0, nz - 1)], ag_send)

    @pl.when(z >= owners)
    def _():
        wait_out(gpart.at[pl.ds(0, owners)], rs_send)

    wait_out(gmr.at[pl.ds(0, nz - 1)], gm_send)
    wait_out(gmx, gmx_send)


def per_device(nt, nz, hidden, tenant_ids, base_weight, adapter_in, adapter_out, magnitude, cotangent):
    tok, ffl = hidden.shape
    adapt = adapter_in.shape[1]
    tenants = magnitude.shape[0]
    rank = adapt // tenants
    tiles = (ffl // 128 + 2) * (rank // 8)
    per = 3
    while tiles > per * nz:
        per += 1
    while tiles % per:
        per += 1
    part_rows = -(-8 * per // 16) * 16
    vmem = pl.BlockSpec(memory_space=pltpu.VMEM)
    hbm = pl.BlockSpec(memory_space=pl.ANY)
    dma = pltpu.SemaphoreType.DMA
    tile = (8, 128)
    scratch = [
        pltpu.VMEM((ffl, adapt), bf16),
        pltpu.VMEM((adapt, 256), bf16),
        pltpu.VMEM((tenants, 256), f32),
        pltpu.VMEM((tok, 256), bf16),
        pltpu.VMEM((nz, ffl, 128), bf16),
        pltpu.VMEM((2, tok, ffl), bf16),
        pltpu.VMEM((adapt, 128), bf16),
        pltpu.VMEM((nt, adapt, 128), bf16),
        pltpu.VMEM((rank, tok), bf16),
        pltpu.VMEM((nt, rank, tok), bf16),
        pltpu.VMEM((rank, tok), bf16),
        pltpu.VMEM((nt, rank, tok), bf16),
        pltpu.VMEM(tile, f32),
        pltpu.VMEM((2 * nz,) + tile, f32),
        pltpu.VMEM(tile, f32),
        pltpu.VMEM((2,) + tile, f32),
        pltpu.VMEM((tok, 256), bf16),
        pltpu.VMEM((nt, tok, 256), bf16),
        pltpu.VMEM((nz, tok, 128), f32),
        pltpu.VMEM((nz, tok, 128), bf16),
        pltpu.VMEM((nz, tok, 128), bf16),
        pltpu.VMEM((nz, tok, 128), bf16),
        pltpu.VMEM((nt, tok, 128), bf16),
        pltpu.VMEM((2, tok, ffl), f32),
        pltpu.VMEM((tok, ffl), bf16),
        pltpu.VMEM((tok, ffl), bf16),
        pltpu.VMEM((nz, part_rows, 128), bf16),
        pltpu.VMEM((nz, part_rows, 128), bf16),
        pltpu.VMEM((tenants * per * 8, 128), f32),
        pltpu.VMEM((tenants * per * 8, 128), f32),
        pltpu.VMEM((nz, tenants * per * 8, 128), bf16),
        pltpu.VMEM((adapt, ffl), f32),
        pltpu.VMEM(tile, f32),
        pltpu.VMEM((nz,) + tile, f32),
        pltpu.VMEM(tile, f32),
        pltpu.VMEM(tile, f32),
        dma((6,)), dma, dma((nz,)), dma((nz,)), dma, dma, dma, dma,
        dma, dma, dma, dma, dma, dma, dma, dma((2,)),
        dma, dma((nt,)), dma, dma, dma((nz,)), dma, dma, dma, dma,
        dma, dma, dma, dma, dma, dma, dma, dma, dma, dma,
    ]
    return pl.pallas_call(
        functools.partial(kernel, nt=nt, nz=nz),
        out_shape=(
            jax.ShapeDtypeStruct((tok, 256), bf16),
            jax.ShapeDtypeStruct((tok, ffl), bf16),
            jax.ShapeDtypeStruct((ffl, adapt), f32),
            jax.ShapeDtypeStruct((adapt, 256), f32),
            jax.ShapeDtypeStruct(magnitude.shape, f32),
        ),
        in_specs=[hbm, pl.BlockSpec(memory_space=pltpu.SMEM)] + [hbm] * 5,
        out_specs=[vmem] * 5,
        scratch_shapes=scratch,
        compiler_params=pltpu.CompilerParams(
            collective_id=0, has_side_effects=True, vmem_limit_bytes=48 * 2**20
        ),
        name="dora",
    )(hidden, tenant_ids, base_weight, adapter_in, adapter_out, magnitude, cotangent)


def solution(mesh):
    nt = mesh.shape["tensor"]
    nz = mesh.shape["dp"] // 2
    return jax.shard_map(
        functools.partial(per_device, nt, nz),
        mesh=mesh,
        in_specs=(
            P("dp", "tensor"),
            P(),
            P("tensor", "dp"),
            P("tensor", None),
            P(None, "tensor"),
            P(None, "tensor"),
            P("dp", "tensor"),
        ),
        out_specs=(
            P("dp", "tensor"),
            P("dp", "tensor"),
            P("tensor", None),
            P(None, "tensor"),
            P(None, "tensor"),
        ),
        check_vma=False,
    )
```

```python
import functools

import jax
import jax.numpy as jnp
from jax import lax
from jax.experimental import pallas as pl
from jax.experimental.pallas import tpu as pltpu
from jax.sharding import PartitionSpec as P

epsilon = 1e-06
f32 = jnp.float32
bf16 = jnp.bfloat16
MESH = pl.DeviceIdType.MESH


def dot(lhs, rhs, lhs_dim, rhs_dim, precision=None):
    return lax.dot_general(
        lhs,
        rhs,
        (((lhs_dim,), (rhs_dim,)), ((), ())),
        precision=precision,
        preferred_element_type=f32,
    )


def loop(count, body):
    lax.fori_loop(0, count, lambda i, c: (body(i), c)[1], 0)


def kernel(
    h_hbm, tid, w_hbm, a_hbm, o_hbm, mag_hbm, cot_hbm,
    adapted, ig, gin, gout, gmag,
    a, o, mag, cot, wbuf, hbuf, ob, obd, lrs, lrr, bas, bar, sqs, sqr, sqb, sqf, slb, gbuf,
    cacc, sst, srecv, cst, crecv, igacc, igs, igr, gpart, grecv, gres, agd, gt,
    gms, gmr, gmx, gmxr,
    in_sem, ring_send, ring_right, ring_left, h_send, h_recv, o_send, o_recv,
    lr_send, lr_recv, ba_send, ba_recv, s1_send, s1_recv, s2_send, s2_recv,
    g_send, g_recv, f_send, sib_send, sib_recv, c_send, c_recv, ig_send, ig_recv,
    rs_send, rs_recv, gx_send, gx_recv, ag_send, ag_recv, gm_send, gm_recv, gmx_send, gmx_recv,
    *, nt, nz,
):
    tok, ffl = igs.shape
    adapt = a.shape[1]
    tenants = mag.shape[0]
    rank = adapt // tenants
    nm = nt // 2
    far = nz // 2
    half_rows = ffl // 2
    d = lax.axis_index("dp")
    t = lax.axis_index("tensor")
    yl = d // nz
    z = d % nz
    core = t % 2
    pair = (1 - yl) * nz + z
    sibling = t + 1 - 2 * core
    mine = t % nm
    plane = t // nm
    in_plane = plane == yl

    def remote(src, dst, send, recv, dp, tensor):
        return pltpu.make_async_remote_copy(
            src_ref=src, dst_ref=dst, send_sem=send, recv_sem=recv,
            device_id=(dp, tensor), device_id_type=MESH,
        )

    def wait_in(ref, sem):
        pltpu.make_async_copy(ref, ref, sem).wait()

    wait_out = wait_in

    loads = [
        pltpu.make_async_copy(src, dst, in_sem.at[i])
        for i, (src, dst) in enumerate((
            (w_hbm, wbuf.at[z]), (h_hbm, hbuf.at[yl]), (a_hbm, a), (o_hbm, o),
            (mag_hbm, mag), (cot_hbm, cot),
        ))
    ]
    for load in loads:
        load.start()

    barrier = pltpu.get_barrier_semaphore()

    def greet_plane(i):
        s = i // nt
        u = i % nt

        @pl.when((s != yl) | (u != t))
        def _():
            pl.semaphore_signal(barrier, inc=1, device_id=(s * nz + z, u), device_id_type=MESH)

    def greet_column(i):
        @pl.when(i % nz != z)
        def _():
            pl.semaphore_signal(barrier, inc=1, device_id=(i, t), device_id_type=MESH)

    loop(2 * nt, greet_plane)
    loop(2 * nz, greet_column)
    for load in loads:
        load.wait()
    pl.semaphore_wait(barrier, 2 * nt - 1 + 2 * (nz - 1))

    def ring(slot, half, step, right):
        rows = pl.ds(half * half_rows, half_rows)
        to = (z + (1 if right else nz - 1)) % nz
        sems = ring_right if right else ring_left
        ref = wbuf.at[slot, rows]
        return remote(ref, ref, ring_send, sems.at[(step - 1) * 2 + half], yl * nz + to, t)

    def carried(step, half, right):
        return step < far or half == (0 if right else 1)

    def ring_step(step):
        for half in (0, 1):
            for right in (True, False):
                if not carried(step, half, right):
                    continue
                slot = (z + (nz - step if right else step)) % nz
                ring(slot, half, step, right).wait_recv()
                if step < far and carried(step + 1, half, right):
                    ring(slot, half, step + 1, right).start()

    for half in (0, 1):
        for right in (True, False):
            if carried(1, half, right):
                ring(z, half, 1, right).start()

    lead = d // 2
    ocols = pl.ds(pl.multiple_of((z % 2) * 128, 128), 128)

    @pl.when(t == lead)
    def _():
        ob[...] = o[:, ocols]

        def send(u):
            @pl.when(u != t)
            def _():
                remote(ob, ob, o_send, o_recv, d, u).start()

        loop(nt, send)

    tenant = tid[d // 2]

    owner = lax.div(lax.broadcasted_iota(jnp.int32, (tok, adapt), 1), rank)
    turned = jnp.where(owner == tenant, dot(hbuf[yl], a[...], 1, 0), 0.0).T
    packed = turned[0:rank]
    for k in range(1, tenants):
        packed = packed + turned[k * rank:(k + 1) * rank]
    lrs[...] = packed.astype(bf16)

    def send_lr(u):
        @pl.when(u != t)
        def _():
            remote(lrs, lrr.at[t], lr_send, lr_recv, d, u).start()

    grow = lax.div(lax.broadcasted_iota(jnp.int32, (adapt, adapt), 0), rank)
    gcol = lax.div(lax.broadcasted_iota(jnp.int32, (adapt, adapt), 1), rank)
    gram = jnp.where(grow == gcol, dot(a[...], a[...], 0, 0), 0.0)
    cross = dot(a[...], wbuf[z], 0, 0)
    wide = wbuf[z].astype(f32)
    column_sq = jnp.sum(wide * wide, axis=0, keepdims=True)

    @pl.when(t != lead)
    def _():
        wait_in(ob, o_recv)

    own = ob[...].astype(f32)
    inner = dot(gram, own, 1, 0, lax.Precision.HIGHEST)
    prod = (2.0 * cross + inner) * own
    rows = [
        jnp.sum(prod[k * rank:(k + 1) * rank], axis=0, keepdims=True) + column_sq
        for k in range(tenants)
    ]
    sqs[...] = jnp.concatenate(rows + [jnp.zeros((8 - tenants, 128), f32)], axis=0)

    @pl.when(t != lead)
    def _():
        remote(sqs, sqr.at[t], s1_send, s1_recv, d, lead).start()

    @pl.when(t == lead)
    def _():
        sqr[t] = sqs[...]

    ring_step(1)
    remote(hbuf.at[yl], hbuf.at[yl], h_send, h_recv, pair, t).start()

    @pl.when(t == lead)
    def _():
        wait_in(sqr.at[pl.ds(0, nt - 1)], s1_recv)
        total = sqr[0]
        for u in range(1, nt):
            total = total + sqr[u]
        sqb[...] = total

        def send(i):
            to = (i % 2) * nz + (z + far + (i // 4) * (1 - (i // 2) % 2 * 2) + nz - (i // 2) % 2) % nz

            @pl.when(to != d)
            def _():
                remote(sqb, sqf.at[d % 2], s2_send, s2_recv.at[d % 2], to, t).start()

        loop(2 * nz, send)
        sqf[d % 2] = total

    loop(nt, send_lr)
    lrr[t] = lrs[...]
    if far > 2:
        ring_step(2)

    def share(b):
        sst[b] = dot(hbuf[1 - core], wbuf[b], 1, 0).astype(bf16)
        remote(sst.at[b], srecv.at[b], sib_send, sib_recv.at[b], d, sibling).start()
        cacc[b] = dot(hbuf[core], wbuf[b], 1, 0)

    def deliver(b):
        m = b // 2
        place = (t // 2) * 2 + b % 2
        wait_in(srecv.at[b], sib_recv.at[b])
        cst[b] = (cacc[b] + srecv[b].astype(f32)).astype(bf16)
        here = (core == yl) & in_plane & (m == mine)

        @pl.when(here)
        def _():
            crecv[place] = cst[b]

        @pl.when(jnp.logical_not(here))
        def _():
            remote(
                cst.at[b], crecv.at[place], c_send, c_recv, core * nz + z, yl * nm + m
            ).start()

    def near(step):
        return 2 * step + 1, lambda i: (z + nz - step + i) % nz

    def at(step):
        return 2, lambda i: (z + step + i * (2 * nz - 2 * step)) % nz

    def each(blocks, body):
        loop(blocks[0], lambda i: body(blocks[1](i)))

    ready = min(3, far - 1)
    if far > 3:
        ring_step(3)

    for e in (0, 1):
        @pl.when(d != 2 * t + e)
        def _(e=e):
            wait_in(sqf.at[e], s2_recv.at[e])

    squares = jnp.concatenate([sqf[0], sqf[1]], axis=1)[0:tenants]
    length = jnp.sqrt(squares + epsilon)
    col_scale = mag[...] / length
    one_hot = lax.broadcasted_iota(jnp.int32, (tenants, 256), 0) == tenant
    scale = jnp.sum(jnp.where(one_hot, col_scale, 0.0), axis=0, keepdims=True)
    slb[...] = (cot[...].astype(f32) * scale).astype(bf16)
    slot = mine * 2 + yl

    def send_slopes(q):
        u = 2 * q + core

        @pl.when(jnp.logical_not(in_plane) | (u != t))
        def _():
            remote(slb, gbuf.at[slot], g_send, g_recv.at[slot], plane * nz + z, u).start()

    loop(nt // 2, send_slopes)

    @pl.when(in_plane)
    def _():
        gbuf[slot] = slb[...]

    out_ten = jnp.zeros((rank, 256), f32)
    for k in range(tenants):
        out_ten = jnp.where(tenant == k, o[k * rank:(k + 1) * rank].astype(f32), out_ten)
    out_ten = out_ten.astype(bf16)
    bas[...] = dot(out_ten, slb[...], 1, 1).astype(bf16)

    def send_back(u):
        @pl.when(u != t)
        def _():
            remote(bas, bar.at[t], ba_send, ba_recv, d, u).start()

    loop(nt, send_back)
    bar[t] = bas[...]

    if far > 4:
        ring_step(4)
    wait_in(hbuf.at[1 - yl], h_recv)
    each(near(ready), share)
    if far > 5:
        ring_step(5)
    each(near(ready), deliver)
    for step in range(ready + 1, min(far, 6)):
        each(at(step), share)
    if far > 6:
        ring_step(6)
        for step in range(ready + 1, 6):
            each(at(step), deliver)
        each(at(6), share)

    wait_in(bar.at[pl.ds(0, nt - 1)], ba_recv)
    back = bar[0].astype(f32)
    for u in range(1, nt):
        back = back + bar[u].astype(f32)
    wait_in(lrr.at[pl.ds(0, nt - 1)], lr_recv)
    low = lrr[0].astype(f32)
    for u in range(1, nt):
        low = low + lrr[u].astype(f32)
    low_high = low.astype(bf16)
    low_rest = (low - low_high.astype(f32)).astype(bf16)
    back_high = back.astype(bf16)
    back_rest = (back - back_high.astype(f32)).astype(bf16)
    grads = [
        dot(back_high, hbuf[yl], 1, 0) + dot(back_rest, hbuf[yl], 1, 0),
        dot(low_high, slb[...], 1, 0) + dot(low_rest, slb[...], 1, 0),
    ]
    tiles = []
    for grad in grads:
        for j in range(grad.shape[1] // 128):
            for g in range(rank // 8):
                tiles.append(grad[g * 8:(g + 1) * 8, j * 128:(j + 1) * 128])
    per = gpart.shape[1] // 8
    owners = len(tiles) // per
    rank_of = 2 * z + yl
    owns = rank_of < owners
    for i in range(owners):
        gpart[i] = jnp.concatenate(tiles[i * per:(i + 1) * per], axis=0).astype(bf16)

    def scatter(i):
        to = (i % 2) * nz + i // 2

        @pl.when(to != d)
        def _():
            remote(gpart.at[i], grecv.at[d], rs_send, rs_recv, to, t).start()

    loop(owners, scatter)

    @pl.when(owns)
    def _():
        grecv[d] = gpart[rank_of]

    if far > 7:
        ring_step(7)
        each(at(6), deliver)
        each(at(7), share)

    row_owner = lax.div(lax.broadcasted_iota(jnp.int32, (adapt, tok), 0), rank)
    full = jnp.where(row_owner == tenant, jnp.concatenate([back] * tenants, axis=0), 0.0)
    igacc[yl] = dot(full.T.astype(bf16), a[...], 1, 1)
    igacc[1 - yl] = jnp.zeros((tok, ffl), f32)
    low_out = dot(low_high, out_ten, 0, 0) + dot(low_rest, out_ten, 0, 0)
    if far > 7:
        each(at(7), deliver)

    ring_step(far)
    share((z + far) % nz)

    held = owners // 2
    ours = pl.ds(yl * held, held)
    theirs = pl.ds((1 - yl) * held, held)

    @pl.when(owns)
    def _():
        wait_in(grecv.at[pl.ds(0, 2 * nz - 1)], rs_recv)
        sums = [jnp.zeros((8 * per, 128), f32)] * tenants
        for i in range(nz):
            both = grecv[2 * i].astype(f32) + grecv[2 * i + 1].astype(f32)
            sums = [acc + jnp.where(tid[i] == k, both, 0.0) for k, acc in enumerate(sums)]
        place = yl * held + z
        gres[place] = jnp.concatenate(sums, axis=0).astype(bf16)

        def spread(i):
            to = (z + far + i) % nz

            @pl.when(to != z)
            def _():
                remote(gres.at[place], gres.at[place], ag_send, ag_recv, yl * nz + to, t).start()

        loop(nz, spread)


    def relay(i):
        at = (2 * (i // 2) + core) * 2 + i % 2

        @pl.when(jnp.logical_not(in_plane) | (at != slot))
        def _():
            wait_in(gbuf.at[at], g_recv.at[at])

        remote(gbuf.at[at], gbuf.at[at], f_send, g_recv.at[at], d, sibling).start()

    def received(i):
        at = (2 * (i // 2) + 1 - core) * 2 + i % 2
        wait_in(gbuf.at[at], g_recv.at[at])

    deliver((z + far) % nz)
    loop(nm, relay)

    loop(nm, received)

    def backward(s):
        def body(m):
            weight = jnp.concatenate([wbuf[2 * m], wbuf[2 * m + 1]], axis=1)
            igacc[s] += dot(gbuf[2 * m + s], weight, 1, 1)

        return body

    loop(nm, backward(1 - yl))
    igs[...] = igacc[1 - yl].astype(bf16)
    remote(igs, igr, ig_send, ig_recv, pair, t).start()

    here = in_plane & (core == yl)

    @pl.when(here)
    def _():
        wait_in(crecv.at[pl.ds(0, nt - 2)], c_recv)

    @pl.when(jnp.logical_not(here))
    def _():
        wait_in(crecv, c_recv)

    sums = []
    for half in (0, 1):
        cols = slice(half * 128, (half + 1) * 128)
        total = low_out[:, cols]
        for q in range(nt // 2):
            total = total + crecv[2 * q + half].astype(f32)
        adapted[:, cols] = (total * scale[:, cols]).astype(bf16)
        sums.append(jnp.sum(cot[:, cols].astype(f32) * total, axis=0, keepdims=True))
    hot = lax.broadcasted_iota(jnp.int32, (tenants, 128), 0) == tenant
    gms[...] = jnp.concatenate([jnp.where(hot, part, 0.0) for part in sums], axis=0)

    def send_mag(i):
        to = (z + far + i) % nz

        @pl.when(to != z)
        def _():
            remote(gms, gmr.at[z], gm_send, gm_recv, yl * nz + to, t).start()

    loop(nz, send_mag)
    gmr[z] = gms[...]

    loop(nm, backward(yl))

    @pl.when(owns)
    def _():
        wait_in(gres.at[pl.ds(0, held - 1)], ag_recv)

    @pl.when(jnp.logical_not(owns))
    def _():
        wait_in(gres.at[ours], ag_recv)

    remote(gres.at[ours], gres.at[ours], gx_send, gx_recv, pair, t).start()
    wait_in(gmr.at[pl.ds(0, nz - 1)], gm_recv)
    total = gmr[0]
    for i in range(1, nz):
        total = total + gmr[i]
    gmx[...] = total
    remote(gmx, gmxr, gmx_send, gmx_recv, pair, t).start()

    wait_in(igr, ig_recv)
    ig[...] = (igacc[yl] + igr[...].astype(f32)).astype(bf16)

    wait_in(gres.at[theirs], gx_recv)
    for i in range(len(tiles)):
        j, g = divmod(i, rank // 8)
        o_index = i // per
        part = gres[o_index % 2 * held + o_index // 2].astype(f32)
        for k in range(tenants):
            row = k * rank + g * 8
            src = (k * per + i % per) * 8
            if j < ffl // 128:
                gt[row:row + 8, j * 128:(j + 1) * 128] = part[src:src + 8]
            else:
                j2 = j - ffl // 128
                gout[row:row + 8, j2 * 128:(j2 + 1) * 128] = part[src:src + 8]
    for j in range(ffl // 128):
        gin[j * 128:(j + 1) * 128] = gt[:, j * 128:(j + 1) * 128].T

    wait_in(gmxr, gmx_recv)
    total = gmx[...] + gmxr[...]
    gmag[...] = jnp.concatenate([total[0:tenants], total[tenants:]], axis=1) / length

    wait_out(wbuf.at[pl.ds(0, nz - 1)], ring_send)
    wait_out(hbuf.at[0], h_send)

    @pl.when(t != lead)
    def _():
        wait_out(sqs, s1_send)

    @pl.when(t == lead)
    def _():
        wait_out(obd.at[pl.ds(0, nt - 1)], o_send)
        wait_out(sqr.at[pl.ds(0, 2 * nz - 1)], s2_send)

    wait_out(lrr.at[pl.ds(0, nt - 1)], lr_send)
    wait_out(bar.at[pl.ds(0, nt - 1)], ba_send)

    @pl.when(in_plane)
    def _():
        wait_out(gbuf.at[pl.ds(0, nt // 2 - 1)], g_send)

    @pl.when(jnp.logical_not(in_plane))
    def _():
        wait_out(gbuf.at[pl.ds(0, nt // 2)], g_send)

    wait_out(gbuf.at[pl.ds(0, nm)], f_send)
    wait_out(sst, sib_send)

    @pl.when(here)
    def _():
        wait_out(cst.at[pl.ds(0, nz - 2)], c_send)

    @pl.when(jnp.logical_not(here))
    def _():
        wait_out(cst, c_send)

    wait_out(igs, ig_send)

    @pl.when(owns)
    def _():
        wait_out(gpart.at[pl.ds(0, owners - 1)], rs_send)
        wait_out(agd.at[pl.ds(0, nz - 1)], ag_send)

    @pl.when(jnp.logical_not(owns))
    def _():
        wait_out(gpart, rs_send)

    wait_out(gres.at[ours], gx_send)
    wait_out(gmr.at[pl.ds(0, nz - 1)], gm_send)
    wait_out(gmx, gmx_send)


def per_device(nt, nz, hidden, tenant_ids, base_weight, adapter_in, adapter_out, magnitude, cotangent):
    tok, ffl = hidden.shape
    adapt = adapter_in.shape[1]
    tenants = magnitude.shape[0]
    rank = adapt // tenants
    tiles = (ffl // 128 + 2) * (rank // 8)
    per = 2
    owners = tiles // per
    vmem = pl.BlockSpec(memory_space=pltpu.VMEM)
    hbm = pl.BlockSpec(memory_space=pl.ANY)
    dma = pltpu.SemaphoreType.DMA
    tile = (8, 128)
    scratch = [
        pltpu.VMEM((ffl, adapt), bf16),
        pltpu.VMEM((adapt, 256), bf16),
        pltpu.VMEM((tenants, 256), f32),
        pltpu.VMEM((tok, 256), bf16),
        pltpu.VMEM((nz, ffl, 128), bf16),
        pltpu.VMEM((2, tok, ffl), bf16),
        pltpu.VMEM((adapt, 128), bf16),
        pltpu.VMEM((nt, adapt, 128), bf16),
        pltpu.VMEM((rank, tok), bf16),
        pltpu.VMEM((nt, rank, tok), bf16),
        pltpu.VMEM((rank, tok), bf16),
        pltpu.VMEM((nt, rank, tok), bf16),
        pltpu.VMEM(tile, f32),
        pltpu.VMEM((2 * nz,) + tile, f32),
        pltpu.VMEM(tile, f32),
        pltpu.VMEM((2,) + tile, f32),
        pltpu.VMEM((tok, 256), bf16),
        pltpu.VMEM((nt, tok, 256), bf16),
        pltpu.VMEM((nz, tok, 128), f32),
        pltpu.VMEM((nz, tok, 128), bf16),
        pltpu.VMEM((nz, tok, 128), bf16),
        pltpu.VMEM((nz, tok, 128), bf16),
        pltpu.VMEM((nt, tok, 128), bf16),
        pltpu.VMEM((2, tok, ffl), f32),
        pltpu.VMEM((tok, ffl), bf16),
        pltpu.VMEM((tok, ffl), bf16),
        pltpu.VMEM((owners, 8 * per, 128), bf16),
        pltpu.VMEM((2 * nz, 8 * per, 128), bf16),
        pltpu.VMEM((owners, tenants * per * 8, 128), bf16),
        pltpu.VMEM((nz, tenants * per * 8, 128), bf16),
        pltpu.VMEM((adapt, ffl), f32),
        pltpu.VMEM(tile, f32),
        pltpu.VMEM((nz,) + tile, f32),
        pltpu.VMEM(tile, f32),
        pltpu.VMEM(tile, f32),
        dma((6,)), dma, dma((nz,)), dma((nz,)), dma, dma, dma, dma,
        dma, dma, dma, dma, dma, dma, dma, dma((2,)),
        dma, dma((nt,)), dma, dma, dma((nz,)), dma, dma, dma, dma,
        dma, dma, dma, dma, dma, dma, dma, dma, dma, dma,
    ]
    return pl.pallas_call(
        functools.partial(kernel, nt=nt, nz=nz),
        out_shape=(
            jax.ShapeDtypeStruct((tok, 256), bf16),
            jax.ShapeDtypeStruct((tok, ffl), bf16),
            jax.ShapeDtypeStruct((ffl, adapt), f32),
            jax.ShapeDtypeStruct((adapt, 256), f32),
            jax.ShapeDtypeStruct(magnitude.shape, f32),
        ),
        in_specs=[hbm, pl.BlockSpec(memory_space=pltpu.SMEM)] + [hbm] * 5,
        out_specs=[vmem] * 5,
        scratch_shapes=scratch,
        compiler_params=pltpu.CompilerParams(
            collective_id=0, has_side_effects=True, vmem_limit_bytes=48 * 2**20
        ),
        name="dora",
    )(hidden, tenant_ids, base_weight, adapter_in, adapter_out, magnitude, cotangent)


def solution(mesh):
    nt = mesh.shape["tensor"]
    nz = mesh.shape["dp"] // 2
    return jax.shard_map(
        functools.partial(per_device, nt, nz),
        mesh=mesh,
        in_specs=(
            P("dp", "tensor"),
            P(),
            P("tensor", "dp"),
            P("tensor", None),
            P(None, "tensor"),
            P(None, "tensor"),
            P("dp", "tensor"),
        ),
        out_specs=(
            P("dp", "tensor"),
            P("dp", "tensor"),
            P("tensor", None),
            P(None, "tensor"),
            P(None, "tensor"),
        ),
        check_vma=False,
    )
```

```python
import functools

import jax
import jax.numpy as jnp
from jax import lax
from jax.experimental import pallas as pl
from jax.experimental.pallas import tpu as pltpu
from jax.sharding import PartitionSpec as P

epsilon = 1e-06
f32 = jnp.float32
bf16 = jnp.bfloat16
MESH = pl.DeviceIdType.MESH


def dot(lhs, rhs, lhs_dim, rhs_dim, precision=None):
    return lax.dot_general(
        lhs,
        rhs,
        (((lhs_dim,), (rhs_dim,)), ((), ())),
        precision=precision,
        preferred_element_type=f32,
    )


def loop(count, body):
    lax.fori_loop(0, count, lambda i, c: (body(i), c)[1], 0)


def kernel(
    h_hbm, tid, w_hbm, a_hbm, o_hbm, mag_hbm, cot_hbm,
    adapted, ig, gin, gout, gmag,
    a, o, mag, cot, wbuf, hbuf, ob, obd, lrs, lrr, bas, bar, sqs, sqr, sqb, sqf, slb, gbuf,
    cacc, sst, srecv, cst, crecv, igacc, igs, igr, gpart, grecv, gres, agd, gt,
    gms, gmr, gmx, gmxr,
    in_sem, ring_send, ring_right, ring_left, h_send, h_recv, o_send, o_recv,
    lr_send, lr_recv, ba_send, ba_recv, s1_send, s1_recv, s2_send, s2_recv,
    g_send, g_recv, f_send, sib_send, sib_recv, c_send, c_recv, ig_send, ig_recv,
    rs_send, rs_recv, gx_send, gx_recv, ag_send, ag_recv, gm_send, gm_recv, gmx_send, gmx_recv,
    *, nt, nz,
):
    tok, ffl = igs.shape
    adapt = a.shape[1]
    tenants = mag.shape[0]
    rank = adapt // tenants
    nm = nt // 2
    far = nz // 2
    half_rows = ffl // 2
    d = lax.axis_index("dp")
    t = lax.axis_index("tensor")
    yl = d // nz
    z = d % nz
    core = t % 2
    pair = (1 - yl) * nz + z
    sibling = t + 1 - 2 * core
    mine = t % nm
    plane = t // nm
    in_plane = plane == yl

    def remote(src, dst, send, recv, dp, tensor):
        return pltpu.make_async_remote_copy(
            src_ref=src, dst_ref=dst, send_sem=send, recv_sem=recv,
            device_id=(dp, tensor), device_id_type=MESH,
        )

    def wait_in(ref, sem):
        pltpu.make_async_copy(ref, ref, sem).wait()

    wait_out = wait_in

    loads = [
        pltpu.make_async_copy(src, dst, in_sem.at[i])
        for i, (src, dst) in enumerate((
            (w_hbm, wbuf.at[z]), (h_hbm, hbuf.at[yl]), (a_hbm, a), (o_hbm, o),
            (mag_hbm, mag), (cot_hbm, cot),
        ))
    ]
    for load in loads:
        load.start()

    barrier = pltpu.get_barrier_semaphore()

    def greet_plane(i):
        s = i // nt
        u = i % nt

        @pl.when((s != yl) | (u != t))
        def _():
            pl.semaphore_signal(barrier, inc=1, device_id=(s * nz + z, u), device_id_type=MESH)

    def greet_column(i):
        @pl.when(i % nz != z)
        def _():
            pl.semaphore_signal(barrier, inc=1, device_id=(i, t), device_id_type=MESH)

    loop(2 * nt, greet_plane)
    loop(2 * nz, greet_column)
    for load in loads:
        load.wait()
    pl.semaphore_wait(barrier, 2 * nt - 1 + 2 * (nz - 1))

    def ring(slot, half, step, right):
        rows = pl.ds(half * half_rows, half_rows)
        to = (z + (1 if right else nz - 1)) % nz
        sems = ring_right if right else ring_left
        ref = wbuf.at[slot, rows]
        return remote(ref, ref, ring_send, sems.at[(step - 1) * 2 + half], yl * nz + to, t)

    def carried(step, half, right):
        return step < far or half == (0 if right else 1)

    def ring_step(step):
        for half in (0, 1):
            for right in (True, False):
                if not carried(step, half, right):
                    continue
                slot = (z + (nz - step if right else step)) % nz
                ring(slot, half, step, right).wait_recv()
                if step < far and carried(step + 1, half, right):
                    ring(slot, half, step + 1, right).start()

    for half in (0, 1):
        for right in (True, False):
            if carried(1, half, right):
                ring(z, half, 1, right).start()

    lead = d // 2
    ocols = pl.ds(pl.multiple_of((z % 2) * 128, 128), 128)

    @pl.when(t == lead)
    def _():
        ob[...] = o[:, ocols]

        def send(u):
            @pl.when(u != t)
            def _():
                remote(ob, ob, o_send, o_recv, d, u).start()

        loop(nt, send)

    tenant = tid[d // 2]

    owner = lax.div(lax.broadcasted_iota(jnp.int32, (tok, adapt), 1), rank)
    turned = jnp.where(owner == tenant, dot(hbuf[yl], a[...], 1, 0), 0.0).T
    packed = turned[0:rank]
    for k in range(1, tenants):
        packed = packed + turned[k * rank:(k + 1) * rank]
    lrs[...] = packed.astype(bf16)

    def send_lr(u):
        @pl.when(u != t)
        def _():
            remote(lrs, lrr.at[t], lr_send, lr_recv, d, u).start()

    grow = lax.div(lax.broadcasted_iota(jnp.int32, (adapt, adapt), 0), rank)
    gcol = lax.div(lax.broadcasted_iota(jnp.int32, (adapt, adapt), 1), rank)
    gram = jnp.where(grow == gcol, dot(a[...], a[...], 0, 0), 0.0)
    cross = dot(a[...], wbuf[z], 0, 0)
    wide = wbuf[z].astype(f32)
    column_sq = jnp.sum(wide * wide, axis=0, keepdims=True)

    @pl.when(t != lead)
    def _():
        wait_in(ob, o_recv)

    own = ob[...].astype(f32)
    inner = dot(gram, own, 1, 0, lax.Precision.HIGHEST)
    prod = (2.0 * cross + inner) * own
    rows = [
        jnp.sum(prod[k * rank:(k + 1) * rank], axis=0, keepdims=True) + column_sq
        for k in range(tenants)
    ]
    sqs[...] = jnp.concatenate(rows + [jnp.zeros((8 - tenants, 128), f32)], axis=0)

    @pl.when(t != lead)
    def _():
        remote(sqs, sqr.at[t], s1_send, s1_recv, d, lead).start()

    @pl.when(t == lead)
    def _():
        sqr[t] = sqs[...]

    ring_step(1)
    remote(hbuf.at[yl], hbuf.at[yl], h_send, h_recv, pair, t).start()

    @pl.when(t == lead)
    def _():
        wait_in(sqr.at[pl.ds(0, nt - 1)], s1_recv)
        total = sqr[0]
        for u in range(1, nt):
            total = total + sqr[u]
        sqb[...] = total

        def send(i):
            to = (i % 2) * nz + (z + far + (i // 4) * (1 - (i // 2) % 2 * 2) + nz - (i // 2) % 2) % nz

            @pl.when(to != d)
            def _():
                remote(sqb, sqf.at[d % 2], s2_send, s2_recv.at[d % 2], to, t).start()

        loop(2 * nz, send)
        sqf[d % 2] = total

    loop(nt, send_lr)
    lrr[t] = lrs[...]
    if far > 2:
        ring_step(2)

    def share(b):
        sst[b] = dot(hbuf[1 - core], wbuf[b], 1, 0).astype(bf16)
        remote(sst.at[b], srecv.at[b], sib_send, sib_recv.at[b], d, sibling).start()
        cacc[b] = dot(hbuf[core], wbuf[b], 1, 0)

    def deliver(b):
        m = b // 2
        place = (t // 2) * 2 + b % 2
        wait_in(srecv.at[b], sib_recv.at[b])
        cst[b] = (cacc[b] + srecv[b].astype(f32)).astype(bf16)
        here = (core == yl) & in_plane & (m == mine)

        @pl.when(here)
        def _():
            crecv[place] = cst[b]

        @pl.when(jnp.logical_not(here))
        def _():
            remote(
                cst.at[b], crecv.at[place], c_send, c_recv, core * nz + z, yl * nm + m
            ).start()

    def near(step):
        return 2 * step + 1, lambda i: (z + nz - step + i) % nz

    def at(step):
        return 2, lambda i: (z + step + i * (2 * nz - 2 * step)) % nz

    def each(blocks, body):
        loop(blocks[0], lambda i: body(blocks[1](i)))

    ready = min(3, far - 1)
    if far > 3:
        ring_step(3)

    for e in (0, 1):
        @pl.when(d != 2 * t + e)
        def _(e=e):
            wait_in(sqf.at[e], s2_recv.at[e])

    squares = jnp.concatenate([sqf[0], sqf[1]], axis=1)[0:tenants]
    length = jnp.sqrt(squares + epsilon)
    col_scale = mag[...] / length
    one_hot = lax.broadcasted_iota(jnp.int32, (tenants, 256), 0) == tenant
    scale = jnp.sum(jnp.where(one_hot, col_scale, 0.0), axis=0, keepdims=True)
    slb[...] = (cot[...].astype(f32) * scale).astype(bf16)
    slot = mine * 2 + yl

    def send_slopes(q):
        u = 2 * q + core

        @pl.when(jnp.logical_not(in_plane) | (u != t))
        def _():
            remote(slb, gbuf.at[slot], g_send, g_recv.at[slot], plane * nz + z, u).start()

    loop(nt // 2, send_slopes)

    @pl.when(in_plane)
    def _():
        gbuf[slot] = slb[...]

    out_ten = jnp.zeros((rank, 256), f32)
    for k in range(tenants):
        out_ten = jnp.where(tenant == k, o[k * rank:(k + 1) * rank].astype(f32), out_ten)
    out_ten = out_ten.astype(bf16)
    bas[...] = dot(out_ten, slb[...], 1, 1).astype(bf16)

    def send_back(u):
        @pl.when(u != t)
        def _():
            remote(bas, bar.at[t], ba_send, ba_recv, d, u).start()

    loop(nt, send_back)
    bar[t] = bas[...]

    if far > 4:
        ring_step(4)
    wait_in(hbuf.at[1 - yl], h_recv)
    each(near(ready), share)
    if far > 5:
        ring_step(5)
    each(near(ready), deliver)
    for step in range(ready + 1, min(far, 6)):
        each(at(step), share)
    if far > 6:
        ring_step(6)
        for step in range(ready + 1, 6):
            each(at(step), deliver)
        each(at(6), share)

    wait_in(bar.at[pl.ds(0, nt - 1)], ba_recv)
    back = bar[0].astype(f32)
    for u in range(1, nt):
        back = back + bar[u].astype(f32)
    wait_in(lrr.at[pl.ds(0, nt - 1)], lr_recv)
    low = lrr[0].astype(f32)
    for u in range(1, nt):
        low = low + lrr[u].astype(f32)
    low_high = low.astype(bf16)
    low_rest = (low - low_high.astype(f32)).astype(bf16)
    back_high = back.astype(bf16)
    back_rest = (back - back_high.astype(f32)).astype(bf16)
    grads = [
        dot(back_high, hbuf[yl], 1, 0) + dot(back_rest, hbuf[yl], 1, 0),
        dot(low_high, slb[...], 1, 0) + dot(low_rest, slb[...], 1, 0),
    ]
    tiles = []
    for grad in grads:
        for j in range(grad.shape[1] // 128):
            for g in range(rank // 8):
                tiles.append(grad[g * 8:(g + 1) * 8, j * 128:(j + 1) * 128])
    per = gpart.shape[1] // 8
    owners = len(tiles) // per
    rank_of = 2 * z + yl
    owns = rank_of < owners
    for i in range(owners):
        gpart[i] = jnp.concatenate(tiles[i * per:(i + 1) * per], axis=0).astype(bf16)

    def scatter(i):
        to = (i % 2) * nz + i // 2

        @pl.when(to != d)
        def _():
            remote(gpart.at[i], grecv.at[d], rs_send, rs_recv, to, t).start()

    loop(owners, scatter)

    @pl.when(owns)
    def _():
        grecv[d] = gpart[rank_of]

    if far > 7:
        ring_step(7)
        each(at(6), deliver)
        each(at(7), share)

    row_owner = lax.div(lax.broadcasted_iota(jnp.int32, (adapt, tok), 0), rank)
    full = jnp.where(row_owner == tenant, jnp.concatenate([back] * tenants, axis=0), 0.0)
    igacc[yl] = dot(full.T.astype(bf16), a[...], 1, 1)
    igacc[1 - yl] = jnp.zeros((tok, ffl), f32)
    low_out = dot(low_high, out_ten, 0, 0) + dot(low_rest, out_ten, 0, 0)
    if far > 7:
        each(at(7), deliver)

    ring_step(far)
    share((z + far) % nz)

    held = owners // 2
    ours = pl.ds(yl * held, held)
    theirs = pl.ds((1 - yl) * held, held)

    @pl.when(owns)
    def _():
        wait_in(grecv.at[pl.ds(0, 2 * nz - 1)], rs_recv)
        sums = [jnp.zeros((8 * per, 128), f32)] * tenants
        for i in range(nz):
            both = grecv[2 * i].astype(f32) + grecv[2 * i + 1].astype(f32)
            sums = [acc + jnp.where(tid[i] == k, both, 0.0) for k, acc in enumerate(sums)]
        place = yl * held + z
        gres[place] = jnp.concatenate(sums, axis=0).astype(bf16)

        def spread(i):
            to = (z + far + i) % nz

            @pl.when(to != z)
            def _():
                remote(gres.at[place], gres.at[place], ag_send, ag_recv, yl * nz + to, t).start()

        loop(nz, spread)


    def relay(i):
        at = (2 * (i // 2) + core) * 2 + i % 2

        @pl.when(jnp.logical_not(in_plane) | (at != slot))
        def _():
            wait_in(gbuf.at[at], g_recv.at[at])

        remote(gbuf.at[at], gbuf.at[at], f_send, g_recv.at[at], d, sibling).start()

    def received(i):
        at = (2 * (i // 2) + 1 - core) * 2 + i % 2
        wait_in(gbuf.at[at], g_recv.at[at])

    deliver((z + far) % nz)
    loop(nm, relay)

    loop(nm, received)

    def backward(s):
        def body(m):
            weight = jnp.concatenate([wbuf[2 * m], wbuf[2 * m + 1]], axis=1)
            igacc[s] += dot(gbuf[2 * m + s], weight, 1, 1)

        return body

    loop(nm, backward(1 - yl))
    igs[...] = igacc[1 - yl].astype(bf16)
    remote(igs, igr, ig_send, ig_recv, pair, t).start()

    here = in_plane & (core == yl)

    @pl.when(here)
    def _():
        wait_in(crecv.at[pl.ds(0, nt - 2)], c_recv)

    @pl.when(jnp.logical_not(here))
    def _():
        wait_in(crecv, c_recv)

    sums = []
    for half in (0, 1):
        cols = slice(half * 128, (half + 1) * 128)
        total = low_out[:, cols]
        for q in range(nt // 2):
            total = total + crecv[2 * q + half].astype(f32)
        adapted[:, cols] = (total * scale[:, cols]).astype(bf16)
        sums.append(jnp.sum(cot[:, cols].astype(f32) * total, axis=0, keepdims=True))
    hot = lax.broadcasted_iota(jnp.int32, (tenants, 128), 0) == tenant
    gms[...] = jnp.concatenate([jnp.where(hot, part, 0.0) for part in sums], axis=0)

    def send_mag(i):
        to = (z + far + i) % nz

        @pl.when(to != z)
        def _():
            remote(gms, gmr.at[z], gm_send, gm_recv, yl * nz + to, t).start()

    loop(nz, send_mag)
    gmr[z] = gms[...]

    loop(nm, backward(yl))

    @pl.when(owns)
    def _():
        wait_in(gres.at[pl.ds(0, held - 1)], ag_recv)

    @pl.when(jnp.logical_not(owns))
    def _():
        wait_in(gres.at[ours], ag_recv)

    remote(gres.at[ours], gres.at[ours], gx_send, gx_recv, pair, t).start()
    wait_in(gmr.at[pl.ds(0, nz - 1)], gm_recv)
    total = gmr[0]
    for i in range(1, nz):
        total = total + gmr[i]
    gmx[...] = total
    remote(gmx, gmxr, gmx_send, gmx_recv, pair, t).start()

    wait_in(igr, ig_recv)
    ig[...] = (igacc[yl] + igr[...].astype(f32)).astype(bf16)

    wait_in(gres.at[theirs], gx_recv)
    for i in range(len(tiles)):
        j, g = divmod(i, rank // 8)
        o_index = i // per
        part = gres[o_index % 2 * held + o_index // 2].astype(f32)
        for k in range(tenants):
            row = k * rank + g * 8
            src = (k * per + i % per) * 8
            if j < ffl // 128:
                gt[row:row + 8, j * 128:(j + 1) * 128] = part[src:src + 8]
            else:
                j2 = j - ffl // 128
                gout[row:row + 8, j2 * 128:(j2 + 1) * 128] = part[src:src + 8]
    for j in range(ffl // 128):
        gin[j * 128:(j + 1) * 128] = gt[:, j * 128:(j + 1) * 128].T

    wait_in(gmxr, gmx_recv)
    total = gmx[...] + gmxr[...]
    gmag[...] = jnp.concatenate([total[0:tenants], total[tenants:]], axis=1) / length

    wait_out(wbuf.at[pl.ds(0, nz - 1)], ring_send)
    wait_out(hbuf.at[0], h_send)

    @pl.when(t != lead)
    def _():
        wait_out(sqs, s1_send)

    @pl.when(t == lead)
    def _():
        wait_out(obd.at[pl.ds(0, nt - 1)], o_send)
        wait_out(sqr.at[pl.ds(0, 2 * nz - 1)], s2_send)

    wait_out(lrr.at[pl.ds(0, nt - 1)], lr_send)
    wait_out(bar.at[pl.ds(0, nt - 1)], ba_send)

    @pl.when(in_plane)
    def _():
        wait_out(gbuf.at[pl.ds(0, nt // 2 - 1)], g_send)

    @pl.when(jnp.logical_not(in_plane))
    def _():
        wait_out(gbuf.at[pl.ds(0, nt // 2)], g_send)

    wait_out(gbuf.at[pl.ds(0, nm)], f_send)
    wait_out(sst, sib_send)

    @pl.when(here)
    def _():
        wait_out(cst.at[pl.ds(0, nz - 2)], c_send)

    @pl.when(jnp.logical_not(here))
    def _():
        wait_out(cst, c_send)

    wait_out(igs, ig_send)

    @pl.when(owns)
    def _():
        wait_out(gpart.at[pl.ds(0, owners - 1)], rs_send)
        wait_out(agd.at[pl.ds(0, nz - 1)], ag_send)

    @pl.when(jnp.logical_not(owns))
    def _():
        wait_out(gpart, rs_send)

    wait_out(gres.at[ours], gx_send)
    wait_out(gmr.at[pl.ds(0, nz - 1)], gm_send)
    wait_out(gmx, gmx_send)


def hand_over(*refs):
    for i in range(5):
        refs[5 + i][...] = refs[i][...]


def per_device(nt, nz, hidden, tenant_ids, base_weight, adapter_in, adapter_out, magnitude, cotangent):
    tok, ffl = hidden.shape
    adapt = adapter_in.shape[1]
    tenants = magnitude.shape[0]
    rank = adapt // tenants
    tiles = (ffl // 128 + 2) * (rank // 8)
    per = 2
    owners = tiles // per
    vmem = pl.BlockSpec(memory_space=pltpu.VMEM)
    hbm = pl.BlockSpec(memory_space=pl.ANY)
    dma = pltpu.SemaphoreType.DMA
    tile = (8, 128)
    scratch = [
        pltpu.VMEM((ffl, adapt), bf16),
        pltpu.VMEM((adapt, 256), bf16),
        pltpu.VMEM((tenants, 256), f32),
        pltpu.VMEM((tok, 256), bf16),
        pltpu.VMEM((nz, ffl, 128), bf16),
        pltpu.VMEM((2, tok, ffl), bf16),
        pltpu.VMEM((adapt, 128), bf16),
        pltpu.VMEM((nt, adapt, 128), bf16),
        pltpu.VMEM((rank, tok), bf16),
        pltpu.VMEM((nt, rank, tok), bf16),
        pltpu.VMEM((rank, tok), bf16),
        pltpu.VMEM((nt, rank, tok), bf16),
        pltpu.VMEM(tile, f32),
        pltpu.VMEM((2 * nz,) + tile, f32),
        pltpu.VMEM(tile, f32),
        pltpu.VMEM((2,) + tile, f32),
        pltpu.VMEM((tok, 256), bf16),
        pltpu.VMEM((nt, tok, 256), bf16),
        pltpu.VMEM((nz, tok, 128), f32),
        pltpu.VMEM((nz, tok, 128), bf16),
        pltpu.VMEM((nz, tok, 128), bf16),
        pltpu.VMEM((nz, tok, 128), bf16),
        pltpu.VMEM((nt, tok, 128), bf16),
        pltpu.VMEM((2, tok, ffl), f32),
        pltpu.VMEM((tok, ffl), bf16),
        pltpu.VMEM((tok, ffl), bf16),
        pltpu.VMEM((owners, 8 * per, 128), bf16),
        pltpu.VMEM((2 * nz, 8 * per, 128), bf16),
        pltpu.VMEM((owners, tenants * per * 8, 128), bf16),
        pltpu.VMEM((nz, tenants * per * 8, 128), bf16),
        pltpu.VMEM((adapt, ffl), f32),
        pltpu.VMEM(tile, f32),
        pltpu.VMEM((nz,) + tile, f32),
        pltpu.VMEM(tile, f32),
        pltpu.VMEM(tile, f32),
        dma((6,)), dma, dma((nz,)), dma((nz,)), dma, dma, dma, dma,
        dma, dma, dma, dma, dma, dma, dma, dma((2,)),
        dma, dma((nt,)), dma, dma, dma((nz,)), dma, dma, dma, dma,
        dma, dma, dma, dma, dma, dma, dma, dma, dma, dma,
    ]
    results = pl.pallas_call(
        functools.partial(kernel, nt=nt, nz=nz),
        out_shape=(
            jax.ShapeDtypeStruct((tok, 256), bf16),
            jax.ShapeDtypeStruct((tok, ffl), bf16),
            jax.ShapeDtypeStruct((ffl, adapt), f32),
            jax.ShapeDtypeStruct((adapt, 256), f32),
            jax.ShapeDtypeStruct(magnitude.shape, f32),
        ),
        in_specs=[hbm, pl.BlockSpec(memory_space=pltpu.SMEM)] + [hbm] * 5,
        out_specs=[vmem] * 5,
        scratch_shapes=scratch,
        compiler_params=pltpu.CompilerParams(
            collective_id=0, has_side_effects=True, vmem_limit_bytes=63 * 2**20
        ),
        name="dora",
    )(hidden, tenant_ids, base_weight, adapter_in, adapter_out, magnitude, cotangent)
    return pl.pallas_call(
        hand_over,
        out_shape=[jax.ShapeDtypeStruct(r.shape, r.dtype) for r in results],
        in_specs=[vmem] * 5,
        out_specs=[vmem] * 5,
        compiler_params=pltpu.CompilerParams(vmem_limit_bytes=63 * 2**20),
        name="hand_over",
    )(*results)


def solution(mesh):
    nt = mesh.shape["tensor"]
    nz = mesh.shape["dp"] // 2
    return jax.shard_map(
        functools.partial(per_device, nt, nz),
        mesh=mesh,
        in_specs=(
            P("dp", "tensor"),
            P(),
            P("tensor", "dp"),
            P("tensor", None),
            P(None, "tensor"),
            P(None, "tensor"),
            P("dp", "tensor"),
        ),
        out_specs=(
            P("dp", "tensor"),
            P("dp", "tensor"),
            P("tensor", None),
            P(None, "tensor"),
            P(None, "tensor"),
        ),
        check_vma=False,
    )
```

```python
import functools

import jax
import jax.numpy as jnp
from jax import lax
from jax.experimental import pallas as pl
from jax.experimental.pallas import tpu as pltpu
from jax.sharding import PartitionSpec as P

epsilon = 1e-06
f32 = jnp.float32
bf16 = jnp.bfloat16
MESH = pl.DeviceIdType.MESH


def dot(lhs, rhs, lhs_dim, rhs_dim, precision=None):
    return lax.dot_general(
        lhs,
        rhs,
        (((lhs_dim,), (rhs_dim,)), ((), ())),
        precision=precision,
        preferred_element_type=f32,
    )


def loop(count, body):
    lax.fori_loop(0, count, lambda i, c: (body(i), c)[1], 0)


def kernel(
    h_hbm, tid, w_hbm, a_hbm, o_hbm, mag_hbm, cot_hbm,
    adapted, ig, gin, gout, gmag,
    a, o, mag, cot, wbuf, hbuf, ob, obd, lrs, lrr, bas, bar, sqs, sqr, sqb, sqf, slb, gbuf,
    cacc, sst, srecv, cst, crecv, igacc, igs, igr, gpart, grecv, gres, agd, gt,
    gms, gmr, gmx, gmxr,
    in_sem, ring_send, ring_right, ring_left, h_send, h_recv, o_send, o_recv,
    lr_send, lr_recv, ba_send, ba_recv, s1_send, s1_recv, s2_send, s2_recv,
    g_send, g_recv, f_send, sib_send, sib_recv, c_send, c_recv, ig_send, ig_recv,
    rs_send, rs_recv, gx_send, gx_recv, ag_send, ag_recv, gm_send, gm_recv, gmx_send, gmx_recv,
    *, nt, nz,
):
    tok, ffl = igs.shape
    adapt = a.shape[1]
    tenants = mag.shape[0]
    rank = adapt // tenants
    nm = nt // 2
    far = nz // 2
    half_rows = ffl // 2
    d = lax.axis_index("dp")
    t = lax.axis_index("tensor")
    yl = d // nz
    z = d % nz
    core = t % 2
    pair = (1 - yl) * nz + z
    sibling = t + 1 - 2 * core
    mine = t % nm
    plane = t // nm
    in_plane = plane == yl

    def remote(src, dst, send, recv, dp, tensor):
        return pltpu.make_async_remote_copy(
            src_ref=src, dst_ref=dst, send_sem=send, recv_sem=recv,
            device_id=(dp, tensor), device_id_type=MESH,
        )

    def wait_in(ref, sem):
        pltpu.make_async_copy(ref, ref, sem).wait()

    wait_out = wait_in

    loads = [
        pltpu.make_async_copy(src, dst, in_sem.at[i])
        for i, (src, dst) in enumerate((
            (w_hbm, wbuf.at[z]), (h_hbm, hbuf.at[yl]), (a_hbm, a), (o_hbm, o),
            (mag_hbm, mag), (cot_hbm, cot),
        ))
    ]
    for load in loads:
        load.start()

    barrier = pltpu.get_barrier_semaphore()

    def greet_plane(i):
        s = i // nt
        u = i % nt

        @pl.when((s != yl) | (u != t))
        def _():
            pl.semaphore_signal(barrier, inc=1, device_id=(s * nz + z, u), device_id_type=MESH)

    def greet_column(i):
        @pl.when(i % nz != z)
        def _():
            pl.semaphore_signal(barrier, inc=1, device_id=(i, t), device_id_type=MESH)

    loop(2 * nt, greet_plane)
    loop(2 * nz, greet_column)
    for load in loads:
        load.wait()
    pl.semaphore_wait(barrier, 2 * nt - 1 + 2 * (nz - 1))

    def ring(slot, half, step, right):
        rows = pl.ds(half * half_rows, half_rows)
        to = (z + (1 if right else nz - 1)) % nz
        sems = ring_right if right else ring_left
        ref = wbuf.at[slot, rows]
        return remote(ref, ref, ring_send, sems.at[(step - 1) * 2 + half], yl * nz + to, t)

    def carried(step, half, right):
        return step < far or half == (0 if right else 1)

    def ring_step(step):
        for half in (0, 1):
            for right in (True, False):
                if not carried(step, half, right):
                    continue
                slot = (z + (nz - step if right else step)) % nz
                ring(slot, half, step, right).wait_recv()
                if step < far and carried(step + 1, half, right):
                    ring(slot, half, step + 1, right).start()

    for half in (0, 1):
        for right in (True, False):
            if carried(1, half, right):
                ring(z, half, 1, right).start()

    lead = d // 2
    ocols = pl.ds(pl.multiple_of((z % 2) * 128, 128), 128)

    @pl.when(t == lead)
    def _():
        ob[...] = o[:, ocols]

        def send(u):
            @pl.when(u != t)
            def _():
                remote(ob, ob, o_send, o_recv, d, u).start()

        loop(nt, send)

    tenant = tid[d // 2]

    owner = lax.div(lax.broadcasted_iota(jnp.int32, (tok, adapt), 1), rank)
    turned = jnp.where(owner == tenant, dot(hbuf[yl], a[...], 1, 0), 0.0).T
    packed = turned[0:rank]
    for k in range(1, tenants):
        packed = packed + turned[k * rank:(k + 1) * rank]
    lrs[...] = packed.astype(bf16)

    def send_lr(u):
        @pl.when(u != t)
        def _():
            remote(lrs, lrr.at[t], lr_send, lr_recv, d, u).start()

    grow = lax.div(lax.broadcasted_iota(jnp.int32, (adapt, adapt), 0), rank)
    gcol = lax.div(lax.broadcasted_iota(jnp.int32, (adapt, adapt), 1), rank)
    gram = jnp.where(grow == gcol, dot(a[...], a[...], 0, 0), 0.0)
    cross = dot(a[...], wbuf[z], 0, 0)
    wide = wbuf[z].astype(f32)
    column_sq = jnp.sum(wide * wide, axis=0, keepdims=True)

    @pl.when(t != lead)
    def _():
        wait_in(ob, o_recv)

    own = ob[...].astype(f32)
    inner = dot(gram, own, 1, 0, lax.Precision.HIGHEST)
    prod = (2.0 * cross + inner) * own
    rows = [
        jnp.sum(prod[k * rank:(k + 1) * rank], axis=0, keepdims=True) + column_sq
        for k in range(tenants)
    ]
    sqs[...] = jnp.concatenate(rows + [jnp.zeros((8 - tenants, 128), f32)], axis=0)

    @pl.when(t != lead)
    def _():
        remote(sqs, sqr.at[t], s1_send, s1_recv, d, lead).start()

    @pl.when(t == lead)
    def _():
        sqr[t] = sqs[...]

    ring_step(1)
    remote(hbuf.at[yl], hbuf.at[yl], h_send, h_recv, pair, t).start()

    @pl.when(t == lead)
    def _():
        wait_in(sqr.at[pl.ds(0, nt - 1)], s1_recv)
        total = sqr[0]
        for u in range(1, nt):
            total = total + sqr[u]
        sqb[...] = total

        def send(i):
            to = (i % 2) * nz + (z + far + (i // 4) * (1 - (i // 2) % 2 * 2) + nz - (i // 2) % 2) % nz

            @pl.when(to != d)
            def _():
                remote(sqb, sqf.at[d % 2], s2_send, s2_recv.at[d % 2], to, t).start()

        loop(2 * nz, send)
        sqf[d % 2] = total

    loop(nt, send_lr)
    lrr[t] = lrs[...]
    if far > 2:
        ring_step(2)

    def share(b):
        sst[b] = dot(hbuf[1 - core], wbuf[b], 1, 0).astype(bf16)
        remote(sst.at[b], srecv.at[b], sib_send, sib_recv.at[b], d, sibling).start()
        cacc[b] = dot(hbuf[core], wbuf[b], 1, 0)

    def deliver(b):
        m = b // 2
        place = (t // 2) * 2 + b % 2
        wait_in(srecv.at[b], sib_recv.at[b])
        cst[b] = (cacc[b] + srecv[b].astype(f32)).astype(bf16)
        here = (core == yl) & in_plane & (m == mine)

        @pl.when(here)
        def _():
            crecv[place] = cst[b]

        @pl.when(jnp.logical_not(here))
        def _():
            remote(
                cst.at[b], crecv.at[place], c_send, c_recv, core * nz + z, yl * nm + m
            ).start()

    def near(step):
        return 2 * step + 1, lambda i: (z + nz - step + i) % nz

    def at(step):
        return 2, lambda i: (z + step + i * (2 * nz - 2 * step)) % nz

    def each(blocks, body):
        loop(blocks[0], lambda i: body(blocks[1](i)))

    ready = min(3, far - 1)

    for e in (0, 1):
        @pl.when(d != 2 * t + e)
        def _(e=e):
            wait_in(sqf.at[e], s2_recv.at[e])

    squares = jnp.concatenate([sqf[0], sqf[1]], axis=1)[0:tenants]
    length = jnp.sqrt(squares + epsilon)
    col_scale = mag[...] / length
    one_hot = lax.broadcasted_iota(jnp.int32, (tenants, 256), 0) == tenant
    scale = jnp.sum(jnp.where(one_hot, col_scale, 0.0), axis=0, keepdims=True)
    slb[...] = (cot[...].astype(f32) * scale).astype(bf16)
    slot = mine * 2 + yl

    def send_slopes(q):
        u = 2 * q + core

        @pl.when(jnp.logical_not(in_plane) | (u != t))
        def _():
            remote(slb, gbuf.at[slot], g_send, g_recv.at[slot], plane * nz + z, u).start()

    loop(nt // 2, send_slopes)

    @pl.when(in_plane)
    def _():
        gbuf[slot] = slb[...]

    out_ten = jnp.zeros((rank, 256), f32)
    for k in range(tenants):
        out_ten = jnp.where(tenant == k, o[k * rank:(k + 1) * rank].astype(f32), out_ten)
    out_ten = out_ten.astype(bf16)
    bas[...] = dot(out_ten, slb[...], 1, 1).astype(bf16)

    def send_back(u):
        @pl.when(u != t)
        def _():
            remote(bas, bar.at[t], ba_send, ba_recv, d, u).start()

    loop(nt, send_back)
    bar[t] = bas[...]

    if far > 3:
        ring_step(3)
    if far > 4:
        ring_step(4)
    wait_in(hbuf.at[1 - yl], h_recv)
    each(near(ready), share)
    if far > 5:
        ring_step(5)
    each(near(ready), deliver)
    for step in range(ready + 1, min(far, 6)):
        each(at(step), share)
    if far > 6:
        ring_step(6)
        for step in range(ready + 1, 6):
            each(at(step), deliver)
        each(at(6), share)

    wait_in(bar.at[pl.ds(0, nt - 1)], ba_recv)
    back = bar[0].astype(f32)
    for u in range(1, nt):
        back = back + bar[u].astype(f32)
    wait_in(lrr.at[pl.ds(0, nt - 1)], lr_recv)
    low = lrr[0].astype(f32)
    for u in range(1, nt):
        low = low + lrr[u].astype(f32)
    low_high = low.astype(bf16)
    low_rest = (low - low_high.astype(f32)).astype(bf16)
    back_high = back.astype(bf16)
    back_rest = (back - back_high.astype(f32)).astype(bf16)
    grads = [
        dot(back_high, hbuf[yl], 1, 0) + dot(back_rest, hbuf[yl], 1, 0),
        dot(low_high, slb[...], 1, 0) + dot(low_rest, slb[...], 1, 0),
    ]
    tiles = []
    for grad in grads:
        for j in range(grad.shape[1] // 128):
            for g in range(rank // 8):
                tiles.append(grad[g * 8:(g + 1) * 8, j * 128:(j + 1) * 128])
    per = gpart.shape[1] // 8
    owners = len(tiles) // per
    rank_of = 2 * z + yl
    owns = rank_of < owners
    for i in range(owners):
        gpart[i] = jnp.concatenate(tiles[i * per:(i + 1) * per], axis=0).astype(bf16)

    def scatter(i):
        to = (i % 2) * nz + i // 2

        @pl.when(to != d)
        def _():
            remote(gpart.at[i], grecv.at[d], rs_send, rs_recv, to, t).start()

    loop(owners, scatter)

    @pl.when(owns)
    def _():
        grecv[d] = gpart[rank_of]

    if far > 7:
        ring_step(7)
        each(at(6), deliver)
        each(at(7), share)

    row_owner = lax.div(lax.broadcasted_iota(jnp.int32, (adapt, tok), 0), rank)
    full = jnp.where(row_owner == tenant, jnp.concatenate([back] * tenants, axis=0), 0.0)
    igacc[yl] = dot(full.T.astype(bf16), a[...], 1, 1)
    igacc[1 - yl] = jnp.zeros((tok, ffl), f32)
    low_out = dot(low_high, out_ten, 0, 0) + dot(low_rest, out_ten, 0, 0)
    if far > 7:
        each(at(7), deliver)

    ring_step(far)
    share((z + far) % nz)

    held = owners // 2
    ours = pl.ds(yl * held, held)
    theirs = pl.ds((1 - yl) * held, held)

    @pl.when(owns)
    def _():
        wait_in(grecv.at[pl.ds(0, 2 * nz - 1)], rs_recv)
        sums = [jnp.zeros((8 * per, 128), f32)] * tenants
        for i in range(nz):
            both = grecv[2 * i].astype(f32) + grecv[2 * i + 1].astype(f32)
            sums = [acc + jnp.where(tid[i] == k, both, 0.0) for k, acc in enumerate(sums)]
        place = yl * held + z
        gres[place] = jnp.concatenate(sums, axis=0).astype(bf16)

        def spread(i):
            to = (z + far + i) % nz

            @pl.when(to != z)
            def _():
                remote(gres.at[place], gres.at[place], ag_send, ag_recv, yl * nz + to, t).start()

        loop(nz, spread)


    def relay(i):
        at = (2 * (i // 2) + core) * 2 + i % 2

        @pl.when(jnp.logical_not(in_plane) | (at != slot))
        def _():
            wait_in(gbuf.at[at], g_recv.at[at])

        remote(gbuf.at[at], gbuf.at[at], f_send, g_recv.at[at], d, sibling).start()

    def received(i):
        at = (2 * (i // 2) + 1 - core) * 2 + i % 2
        wait_in(gbuf.at[at], g_recv.at[at])

    deliver((z + far) % nz)
    loop(nm, relay)

    loop(nm, received)

    def backward(s):
        def body(m):
            weight = jnp.concatenate([wbuf[2 * m], wbuf[2 * m + 1]], axis=1)
            igacc[s] += dot(gbuf[2 * m + s], weight, 1, 1)

        return body

    loop(nm, backward(1 - yl))
    igs[...] = igacc[1 - yl].astype(bf16)
    remote(igs, igr, ig_send, ig_recv, pair, t).start()

    here = in_plane & (core == yl)

    @pl.when(here)
    def _():
        wait_in(crecv.at[pl.ds(0, nt - 2)], c_recv)

    @pl.when(jnp.logical_not(here))
    def _():
        wait_in(crecv, c_recv)

    sums = []
    for half in (0, 1):
        cols = slice(half * 128, (half + 1) * 128)
        total = low_out[:, cols]
        for q in range(nt // 2):
            total = total + crecv[2 * q + half].astype(f32)
        adapted[:, cols] = (total * scale[:, cols]).astype(bf16)
        sums.append(jnp.sum(cot[:, cols].astype(f32) * total, axis=0, keepdims=True))
    hot = lax.broadcasted_iota(jnp.int32, (tenants, 128), 0) == tenant
    gms[...] = jnp.concatenate([jnp.where(hot, part, 0.0) for part in sums], axis=0)

    def send_mag(i):
        to = (z + far + i) % nz

        @pl.when(to != z)
        def _():
            remote(gms, gmr.at[z], gm_send, gm_recv, yl * nz + to, t).start()

    loop(nz, send_mag)
    gmr[z] = gms[...]

    loop(nm, backward(yl))

    @pl.when(owns)
    def _():
        wait_in(gres.at[pl.ds(0, held - 1)], ag_recv)

    @pl.when(jnp.logical_not(owns))
    def _():
        wait_in(gres.at[ours], ag_recv)

    remote(gres.at[ours], gres.at[ours], gx_send, gx_recv, pair, t).start()
    wait_in(gmr.at[pl.ds(0, nz - 1)], gm_recv)
    total = gmr[0]
    for i in range(1, nz):
        total = total + gmr[i]
    gmx[...] = total
    remote(gmx, gmxr, gmx_send, gmx_recv, pair, t).start()

    wait_in(igr, ig_recv)
    ig[...] = (igacc[yl] + igr[...].astype(f32)).astype(bf16)

    wait_in(gres.at[theirs], gx_recv)
    for i in range(len(tiles)):
        j, g = divmod(i, rank // 8)
        o_index = i // per
        part = gres[o_index % 2 * held + o_index // 2].astype(f32)
        for k in range(tenants):
            row = k * rank + g * 8
            src = (k * per + i % per) * 8
            if j < ffl // 128:
                gt[row:row + 8, j * 128:(j + 1) * 128] = part[src:src + 8]
            else:
                j2 = j - ffl // 128
                gout[row:row + 8, j2 * 128:(j2 + 1) * 128] = part[src:src + 8]
    for j in range(ffl // 128):
        gin[j * 128:(j + 1) * 128] = gt[:, j * 128:(j + 1) * 128].T

    wait_in(gmxr, gmx_recv)
    total = gmx[...] + gmxr[...]
    gmag[...] = jnp.concatenate([total[0:tenants], total[tenants:]], axis=1) / length

    wait_out(wbuf.at[pl.ds(0, nz - 1)], ring_send)
    wait_out(hbuf.at[0], h_send)

    @pl.when(t != lead)
    def _():
        wait_out(sqs, s1_send)

    @pl.when(t == lead)
    def _():
        wait_out(obd.at[pl.ds(0, nt - 1)], o_send)
        wait_out(sqr.at[pl.ds(0, 2 * nz - 1)], s2_send)

    wait_out(lrr.at[pl.ds(0, nt - 1)], lr_send)
    wait_out(bar.at[pl.ds(0, nt - 1)], ba_send)

    @pl.when(in_plane)
    def _():
        wait_out(gbuf.at[pl.ds(0, nt // 2 - 1)], g_send)

    @pl.when(jnp.logical_not(in_plane))
    def _():
        wait_out(gbuf.at[pl.ds(0, nt // 2)], g_send)

    wait_out(gbuf.at[pl.ds(0, nm)], f_send)
    wait_out(sst, sib_send)

    @pl.when(here)
    def _():
        wait_out(cst.at[pl.ds(0, nz - 2)], c_send)

    @pl.when(jnp.logical_not(here))
    def _():
        wait_out(cst, c_send)

    wait_out(igs, ig_send)

    @pl.when(owns)
    def _():
        wait_out(gpart.at[pl.ds(0, owners - 1)], rs_send)
        wait_out(agd.at[pl.ds(0, nz - 1)], ag_send)

    @pl.when(jnp.logical_not(owns))
    def _():
        wait_out(gpart, rs_send)

    wait_out(gres.at[ours], gx_send)
    wait_out(gmr.at[pl.ds(0, nz - 1)], gm_send)
    wait_out(gmx, gmx_send)


def hand_over(*refs):
    for i in range(5):
        refs[5 + i][...] = refs[i][...]


def per_device(nt, nz, hidden, tenant_ids, base_weight, adapter_in, adapter_out, magnitude, cotangent):
    tok, ffl = hidden.shape
    adapt = adapter_in.shape[1]
    tenants = magnitude.shape[0]
    rank = adapt // tenants
    tiles = (ffl // 128 + 2) * (rank // 8)
    per = 2
    owners = tiles // per
    vmem = pl.BlockSpec(memory_space=pltpu.VMEM)
    hbm = pl.BlockSpec(memory_space=pl.ANY)
    dma = pltpu.SemaphoreType.DMA
    tile = (8, 128)
    scratch = [
        pltpu.VMEM((ffl, adapt), bf16),
        pltpu.VMEM((adapt, 256), bf16),
        pltpu.VMEM((tenants, 256), f32),
        pltpu.VMEM((tok, 256), bf16),
        pltpu.VMEM((nz, ffl, 128), bf16),
        pltpu.VMEM((2, tok, ffl), bf16),
        pltpu.VMEM((adapt, 128), bf16),
        pltpu.VMEM((nt, adapt, 128), bf16),
        pltpu.VMEM((rank, tok), bf16),
        pltpu.VMEM((nt, rank, tok), bf16),
        pltpu.VMEM((rank, tok), bf16),
        pltpu.VMEM((nt, rank, tok), bf16),
        pltpu.VMEM(tile, f32),
        pltpu.VMEM((2 * nz,) + tile, f32),
        pltpu.VMEM(tile, f32),
        pltpu.VMEM((2,) + tile, f32),
        pltpu.VMEM((tok, 256), bf16),
        pltpu.VMEM((nt, tok, 256), bf16),
        pltpu.VMEM((nz, tok, 128), f32),
        pltpu.VMEM((nz, tok, 128), bf16),
        pltpu.VMEM((nz, tok, 128), bf16),
        pltpu.VMEM((nz, tok, 128), bf16),
        pltpu.VMEM((nt, tok, 128), bf16),
        pltpu.VMEM((2, tok, ffl), f32),
        pltpu.VMEM((tok, ffl), bf16),
        pltpu.VMEM((tok, ffl), bf16),
        pltpu.VMEM((owners, 8 * per, 128), bf16),
        pltpu.VMEM((2 * nz, 8 * per, 128), bf16),
        pltpu.VMEM((owners, tenants * per * 8, 128), bf16),
        pltpu.VMEM((nz, tenants * per * 8, 128), bf16),
        pltpu.VMEM((adapt, ffl), f32),
        pltpu.VMEM(tile, f32),
        pltpu.VMEM((nz,) + tile, f32),
        pltpu.VMEM(tile, f32),
        pltpu.VMEM(tile, f32),
        dma((6,)), dma, dma((nz,)), dma((nz,)), dma, dma, dma, dma,
        dma, dma, dma, dma, dma, dma, dma, dma((2,)),
        dma, dma((nt,)), dma, dma, dma((nz,)), dma, dma, dma, dma,
        dma, dma, dma, dma, dma, dma, dma, dma, dma, dma,
    ]
    results = pl.pallas_call(
        functools.partial(kernel, nt=nt, nz=nz),
        out_shape=(
            jax.ShapeDtypeStruct((tok, 256), bf16),
            jax.ShapeDtypeStruct((tok, ffl), bf16),
            jax.ShapeDtypeStruct((ffl, adapt), f32),
            jax.ShapeDtypeStruct((adapt, 256), f32),
            jax.ShapeDtypeStruct(magnitude.shape, f32),
        ),
        in_specs=[hbm, pl.BlockSpec(memory_space=pltpu.SMEM)] + [hbm] * 5,
        out_specs=[vmem] * 5,
        scratch_shapes=scratch,
        compiler_params=pltpu.CompilerParams(
            collective_id=0, has_side_effects=True, vmem_limit_bytes=63 * 2**20
        ),
        name="dora",
    )(hidden, tenant_ids, base_weight, adapter_in, adapter_out, magnitude, cotangent)
    return pl.pallas_call(
        hand_over,
        out_shape=[jax.ShapeDtypeStruct(r.shape, r.dtype) for r in results],
        in_specs=[vmem] * 5,
        out_specs=[vmem] * 5,
        compiler_params=pltpu.CompilerParams(vmem_limit_bytes=63 * 2**20),
        name="hand_over",
    )(*results)


def solution(mesh):
    nt = mesh.shape["tensor"]
    nz = mesh.shape["dp"] // 2
    return jax.shard_map(
        functools.partial(per_device, nt, nz),
        mesh=mesh,
        in_specs=(
            P("dp", "tensor"),
            P(),
            P("tensor", "dp"),
            P("tensor", None),
            P(None, "tensor"),
            P(None, "tensor"),
            P("dp", "tensor"),
        ),
        out_specs=(
            P("dp", "tensor"),
            P("dp", "tensor"),
            P("tensor", None),
            P(None, "tensor"),
            P(None, "tensor"),
        ),
        check_vma=False,
    )
```

```python
import functools

import jax
import jax.numpy as jnp
from jax import lax
from jax.experimental import pallas as pl
from jax.experimental.pallas import tpu as pltpu
from jax.sharding import PartitionSpec as P

epsilon = 1e-06
f32 = jnp.float32
bf16 = jnp.bfloat16
MESH = pl.DeviceIdType.MESH


def dot(lhs, rhs, lhs_dim, rhs_dim, precision=None):
    return lax.dot_general(
        lhs,
        rhs,
        (((lhs_dim,), (rhs_dim,)), ((), ())),
        precision=precision,
        preferred_element_type=f32,
    )


def loop(count, body):
    lax.fori_loop(0, count, lambda i, c: (body(i), c)[1], 0)


def kernel(
    h_hbm, tid, w_hbm, a_hbm, o_hbm, mag_hbm, cot_hbm,
    adapted, ig, gin, gout, gmag,
    a, o, mag, cot, wbuf, hbuf, ob, obd, lrs, lrr, bas, bar, sqs, sqr, sqb, sqf, slb, gbuf,
    cacc, sst, srecv, cst, crecv, igacc, igs, igr, gpart, grecv, gres, agd, gt,
    gms, gmr, gmx, gmxr,
    in_sem, ring_send, ring_right, ring_left, h_send, h_recv, o_send, o_recv,
    lr_send, lr_recv, ba_send, ba_recv, s1_send, s1_recv, s2_send, s2_recv,
    g_send, g_recv, f_send, sib_send, sib_recv, c_send, c_recv, ig_send, ig_recv,
    rs_send, rs_recv, gx_send, gx_recv, ag_send, ag_recv, gm_send, gm_recv, gmx_send, gmx_recv,
    *, nt, nz,
):
    tok, ffl = igs.shape
    adapt = a.shape[1]
    tenants = mag.shape[0]
    rank = adapt // tenants
    nm = nt // 2
    far = nz // 2
    half_rows = ffl // 2
    d = lax.axis_index("dp")
    t = lax.axis_index("tensor")
    yl = d // nz
    z = d % nz
    core = t % 2
    pair = (1 - yl) * nz + z
    sibling = t + 1 - 2 * core
    mine = t % nm
    plane = t // nm
    in_plane = plane == yl

    def remote(src, dst, send, recv, dp, tensor):
        return pltpu.make_async_remote_copy(
            src_ref=src, dst_ref=dst, send_sem=send, recv_sem=recv,
            device_id=(dp, tensor), device_id_type=MESH,
        )

    def wait_in(ref, sem):
        pltpu.make_async_copy(ref, ref, sem).wait()

    wait_out = wait_in

    loads = [
        pltpu.make_async_copy(src, dst, in_sem.at[i])
        for i, (src, dst) in enumerate((
            (w_hbm, wbuf.at[z]), (h_hbm, hbuf.at[yl]), (a_hbm, a), (o_hbm, o),
            (mag_hbm, mag), (cot_hbm, cot),
        ))
    ]
    for load in loads:
        load.start()

    barrier = pltpu.get_barrier_semaphore()

    def greet_plane(i):
        s = i // nt
        u = i % nt

        @pl.when((s != yl) | (u != t))
        def _():
            pl.semaphore_signal(barrier, inc=1, device_id=(s * nz + z, u), device_id_type=MESH)

    def greet_column(i):
        @pl.when(i % nz != z)
        def _():
            pl.semaphore_signal(barrier, inc=1, device_id=(i, t), device_id_type=MESH)

    loop(2 * nt, greet_plane)
    loop(2 * nz, greet_column)
    for load in loads:
        load.wait()
    pl.semaphore_wait(barrier, 2 * nt - 1 + 2 * (nz - 1))

    def ring(slot, half, step, right):
        rows = pl.ds(half * half_rows, half_rows)
        to = (z + (1 if right else nz - 1)) % nz
        sems = ring_right if right else ring_left
        ref = wbuf.at[slot, rows]
        return remote(ref, ref, ring_send, sems.at[(step - 1) * 2 + half], yl * nz + to, t)

    def carried(step, half, right):
        return step < far or half == (0 if right else 1)

    def ring_step(step):
        for half in (0, 1):
            for right in (True, False):
                if not carried(step, half, right):
                    continue
                slot = (z + (nz - step if right else step)) % nz
                ring(slot, half, step, right).wait_recv()
                if step < far and carried(step + 1, half, right):
                    ring(slot, half, step + 1, right).start()

    for half in (0, 1):
        for right in (True, False):
            if carried(1, half, right):
                ring(z, half, 1, right).start()

    lead = d // 2
    ocols = pl.ds(pl.multiple_of((z % 2) * 128, 128), 128)

    @pl.when(t == lead)
    def _():
        ob[...] = o[:, ocols]

        def send(u):
            @pl.when(u != t)
            def _():
                remote(ob, ob, o_send, o_recv, d, u).start()

        loop(nt, send)

    tenant = tid[d // 2]

    owner = lax.div(lax.broadcasted_iota(jnp.int32, (tok, adapt), 1), rank)
    turned = jnp.where(owner == tenant, dot(hbuf[yl], a[...], 1, 0), 0.0).T
    packed = turned[0:rank]
    for k in range(1, tenants):
        packed = packed + turned[k * rank:(k + 1) * rank]
    lrs[...] = packed.astype(bf16)

    def send_lr(u):
        @pl.when(u != t)
        def _():
            remote(lrs, lrr.at[t], lr_send, lr_recv, d, u).start()

    grow = lax.div(lax.broadcasted_iota(jnp.int32, (adapt, adapt), 0), rank)
    gcol = lax.div(lax.broadcasted_iota(jnp.int32, (adapt, adapt), 1), rank)
    gram = jnp.where(grow == gcol, dot(a[...], a[...], 0, 0), 0.0)
    cross = dot(a[...], wbuf[z], 0, 0)
    wide = wbuf[z].astype(f32)
    column_sq = jnp.sum(wide * wide, axis=0, keepdims=True)

    @pl.when(t != lead)
    def _():
        wait_in(ob, o_recv)

    own = ob[...].astype(f32)
    inner = dot(gram, own, 1, 0, lax.Precision.HIGHEST)
    prod = (2.0 * cross + inner) * own
    rows = [
        jnp.sum(prod[k * rank:(k + 1) * rank], axis=0, keepdims=True) + column_sq
        for k in range(tenants)
    ]
    sqs[...] = jnp.concatenate(rows + [jnp.zeros((8 - tenants, 128), f32)], axis=0)

    @pl.when(t != lead)
    def _():
        remote(sqs, sqr.at[t], s1_send, s1_recv, d, lead).start()

    @pl.when(t == lead)
    def _():
        sqr[t] = sqs[...]

    remote(hbuf.at[yl], hbuf.at[yl], h_send, h_recv, pair, t).start()
    ring_step(1)

    @pl.when(t == lead)
    def _():
        wait_in(sqr.at[pl.ds(0, nt - 1)], s1_recv)
        total = sqr[0]
        for u in range(1, nt):
            total = total + sqr[u]
        sqb[...] = total

        def send(i):
            to = (i % 2) * nz + (z + far + (i // 4) * (1 - (i // 2) % 2 * 2) + nz - (i // 2) % 2) % nz

            @pl.when(to != d)
            def _():
                remote(sqb, sqf.at[d % 2], s2_send, s2_recv.at[d % 2], to, t).start()

        loop(2 * nz, send)
        sqf[d % 2] = total

    loop(nt, send_lr)
    lrr[t] = lrs[...]
    if far > 2:
        ring_step(2)

    def share(b):
        sst[b] = dot(hbuf[1 - core], wbuf[b], 1, 0).astype(bf16)
        remote(sst.at[b], srecv.at[b], sib_send, sib_recv.at[b], d, sibling).start()
        cacc[b] = dot(hbuf[core], wbuf[b], 1, 0)

    def deliver(b):
        m = b // 2
        place = (t // 2) * 2 + b % 2
        wait_in(srecv.at[b], sib_recv.at[b])
        cst[b] = (cacc[b] + srecv[b].astype(f32)).astype(bf16)
        here = (core == yl) & in_plane & (m == mine)

        @pl.when(here)
        def _():
            crecv[place] = cst[b]

        @pl.when(jnp.logical_not(here))
        def _():
            remote(
                cst.at[b], crecv.at[place], c_send, c_recv, core * nz + z, yl * nm + m
            ).start()

    def near(step):
        return 2 * step + 1, lambda i: (z + nz - step + i) % nz

    def at(step):
        return 2, lambda i: (z + step + i * (2 * nz - 2 * step)) % nz

    def each(blocks, body):
        loop(blocks[0], lambda i: body(blocks[1](i)))

    ready = min(3, far - 1)

    for e in (0, 1):
        @pl.when(d != 2 * t + e)
        def _(e=e):
            wait_in(sqf.at[e], s2_recv.at[e])

    squares = jnp.concatenate([sqf[0], sqf[1]], axis=1)[0:tenants]
    length = jnp.sqrt(squares + epsilon)
    col_scale = mag[...] / length
    one_hot = lax.broadcasted_iota(jnp.int32, (tenants, 256), 0) == tenant
    scale = jnp.sum(jnp.where(one_hot, col_scale, 0.0), axis=0, keepdims=True)
    slb[...] = (cot[...].astype(f32) * scale).astype(bf16)
    slot = mine * 2 + yl

    def send_slopes(q):
        u = 2 * q + core

        @pl.when(jnp.logical_not(in_plane) | (u != t))
        def _():
            remote(slb, gbuf.at[slot], g_send, g_recv.at[slot], plane * nz + z, u).start()

    loop(nt // 2, send_slopes)

    @pl.when(in_plane)
    def _():
        gbuf[slot] = slb[...]

    out_ten = jnp.zeros((rank, 256), f32)
    for k in range(tenants):
        out_ten = jnp.where(tenant == k, o[k * rank:(k + 1) * rank].astype(f32), out_ten)
    out_ten = out_ten.astype(bf16)
    bas[...] = dot(out_ten, slb[...], 1, 1).astype(bf16)

    def send_back(u):
        @pl.when(u != t)
        def _():
            remote(bas, bar.at[t], ba_send, ba_recv, d, u).start()

    loop(nt, send_back)
    bar[t] = bas[...]

    if far > 3:
        ring_step(3)
    if far > 4:
        ring_step(4)
    wait_in(hbuf.at[1 - yl], h_recv)
    each(near(ready), share)
    if far > 5:
        ring_step(5)
    each(near(ready), deliver)
    for step in range(ready + 1, min(far, 6)):
        each(at(step), share)
    if far > 6:
        ring_step(6)
        for step in range(ready + 1, 6):
            each(at(step), deliver)
        each(at(6), share)

    wait_in(bar.at[pl.ds(0, nt - 1)], ba_recv)
    back = bar[0].astype(f32)
    for u in range(1, nt):
        back = back + bar[u].astype(f32)
    wait_in(lrr.at[pl.ds(0, nt - 1)], lr_recv)
    low = lrr[0].astype(f32)
    for u in range(1, nt):
        low = low + lrr[u].astype(f32)
    low_high = low.astype(bf16)
    low_rest = (low - low_high.astype(f32)).astype(bf16)
    back_high = back.astype(bf16)
    back_rest = (back - back_high.astype(f32)).astype(bf16)
    grads = [
        dot(back_high, hbuf[yl], 1, 0) + dot(back_rest, hbuf[yl], 1, 0),
        dot(low_high, slb[...], 1, 0) + dot(low_rest, slb[...], 1, 0),
    ]
    tiles = []
    for grad in grads:
        for j in range(grad.shape[1] // 128):
            for g in range(rank // 8):
                tiles.append(grad[g * 8:(g + 1) * 8, j * 128:(j + 1) * 128])
    per = gpart.shape[1] // 8
    owners = len(tiles) // per
    rank_of = 2 * z + yl
    owns = rank_of < owners
    for i in range(owners):
        gpart[i] = jnp.concatenate(tiles[i * per:(i + 1) * per], axis=0).astype(bf16)

    def scatter(i):
        to = (i % 2) * nz + i // 2

        @pl.when(to != d)
        def _():
            remote(gpart.at[i], grecv.at[d], rs_send, rs_recv, to, t).start()

    loop(owners, scatter)

    @pl.when(owns)
    def _():
        grecv[d] = gpart[rank_of]

    if far > 7:
        ring_step(7)
        each(at(6), deliver)
        each(at(7), share)

    row_owner = lax.div(lax.broadcasted_iota(jnp.int32, (adapt, tok), 0), rank)
    full = jnp.where(row_owner == tenant, jnp.concatenate([back] * tenants, axis=0), 0.0)
    igacc[yl] = dot(full.T.astype(bf16), a[...], 1, 1)
    igacc[1 - yl] = jnp.zeros((tok, ffl), f32)
    low_out = dot(low_high, out_ten, 0, 0) + dot(low_rest, out_ten, 0, 0)
    if far > 7:
        each(at(7), deliver)

    ring_step(far)
    share((z + far) % nz)

    held = owners // 2
    ours = pl.ds(yl * held, held)
    theirs = pl.ds((1 - yl) * held, held)

    @pl.when(owns)
    def _():
        wait_in(grecv.at[pl.ds(0, 2 * nz - 1)], rs_recv)
        sums = [jnp.zeros((8 * per, 128), f32)] * tenants
        for i in range(nz):
            both = grecv[2 * i].astype(f32) + grecv[2 * i + 1].astype(f32)
            sums = [acc + jnp.where(tid[i] == k, both, 0.0) for k, acc in enumerate(sums)]
        place = yl * held + z
        gres[place] = jnp.concatenate(sums, axis=0).astype(bf16)

        def spread(i):
            to = (z + far + i) % nz

            @pl.when(to != z)
            def _():
                remote(gres.at[place], gres.at[place], ag_send, ag_recv, yl * nz + to, t).start()

        loop(nz, spread)


    def relay(i):
        at = (2 * (i // 2) + core) * 2 + i % 2

        @pl.when(jnp.logical_not(in_plane) | (at != slot))
        def _():
            wait_in(gbuf.at[at], g_recv.at[at])

        remote(gbuf.at[at], gbuf.at[at], f_send, g_recv.at[at], d, sibling).start()

    def received(i):
        at = (2 * (i // 2) + 1 - core) * 2 + i % 2
        wait_in(gbuf.at[at], g_recv.at[at])

    deliver((z + far) % nz)
    loop(nm, relay)

    loop(nm, received)

    def backward(s):
        def body(m):
            weight = jnp.concatenate([wbuf[2 * m], wbuf[2 * m + 1]], axis=1)
            igacc[s] += dot(gbuf[2 * m + s], weight, 1, 1)

        return body

    loop(nm, backward(1 - yl))
    igs[...] = igacc[1 - yl].astype(bf16)
    remote(igs, igr, ig_send, ig_recv, pair, t).start()

    here = in_plane & (core == yl)

    @pl.when(here)
    def _():
        wait_in(crecv.at[pl.ds(0, nt - 2)], c_recv)

    @pl.when(jnp.logical_not(here))
    def _():
        wait_in(crecv, c_recv)

    sums = []
    for half in (0, 1):
        cols = slice(half * 128, (half + 1) * 128)
        total = low_out[:, cols]
        for q in range(nt // 2):
            total = total + crecv[2 * q + half].astype(f32)
        adapted[:, cols] = (total * scale[:, cols]).astype(bf16)
        sums.append(jnp.sum(cot[:, cols].astype(f32) * total, axis=0, keepdims=True))
    hot = lax.broadcasted_iota(jnp.int32, (tenants, 128), 0) == tenant
    gms[...] = jnp.concatenate([jnp.where(hot, part, 0.0) for part in sums], axis=0)

    def send_mag(i):
        to = (z + far + i) % nz

        @pl.when(to != z)
        def _():
            remote(gms, gmr.at[z], gm_send, gm_recv, yl * nz + to, t).start()

    loop(nz, send_mag)
    gmr[z] = gms[...]

    loop(nm, backward(yl))

    @pl.when(owns)
    def _():
        wait_in(gres.at[pl.ds(0, held - 1)], ag_recv)

    @pl.when(jnp.logical_not(owns))
    def _():
        wait_in(gres.at[ours], ag_recv)

    remote(gres.at[ours], gres.at[ours], gx_send, gx_recv, pair, t).start()
    wait_in(gmr.at[pl.ds(0, nz - 1)], gm_recv)
    total = gmr[0]
    for i in range(1, nz):
        total = total + gmr[i]
    gmx[...] = total
    remote(gmx, gmxr, gmx_send, gmx_recv, pair, t).start()

    wait_in(igr, ig_recv)
    ig[...] = (igacc[yl] + igr[...].astype(f32)).astype(bf16)

    wait_in(gres.at[theirs], gx_recv)
    for i in range(len(tiles)):
        j, g = divmod(i, rank // 8)
        o_index = i // per
        part = gres[o_index % 2 * held + o_index // 2].astype(f32)
        for k in range(tenants):
            row = k * rank + g * 8
            src = (k * per + i % per) * 8
            if j < ffl // 128:
                gt[row:row + 8, j * 128:(j + 1) * 128] = part[src:src + 8]
            else:
                j2 = j - ffl // 128
                gout[row:row + 8, j2 * 128:(j2 + 1) * 128] = part[src:src + 8]
    for j in range(ffl // 128):
        gin[j * 128:(j + 1) * 128] = gt[:, j * 128:(j + 1) * 128].T

    wait_in(gmxr, gmx_recv)
    total = gmx[...] + gmxr[...]
    gmag[...] = jnp.concatenate([total[0:tenants], total[tenants:]], axis=1) / length

    wait_out(wbuf.at[pl.ds(0, nz - 1)], ring_send)
    wait_out(hbuf.at[0], h_send)

    @pl.when(t != lead)
    def _():
        wait_out(sqs, s1_send)

    @pl.when(t == lead)
    def _():
        wait_out(obd.at[pl.ds(0, nt - 1)], o_send)
        wait_out(sqr.at[pl.ds(0, 2 * nz - 1)], s2_send)

    wait_out(lrr.at[pl.ds(0, nt - 1)], lr_send)
    wait_out(bar.at[pl.ds(0, nt - 1)], ba_send)

    @pl.when(in_plane)
    def _():
        wait_out(gbuf.at[pl.ds(0, nt // 2 - 1)], g_send)

    @pl.when(jnp.logical_not(in_plane))
    def _():
        wait_out(gbuf.at[pl.ds(0, nt // 2)], g_send)

    wait_out(gbuf.at[pl.ds(0, nm)], f_send)
    wait_out(sst, sib_send)

    @pl.when(here)
    def _():
        wait_out(cst.at[pl.ds(0, nz - 2)], c_send)

    @pl.when(jnp.logical_not(here))
    def _():
        wait_out(cst, c_send)

    wait_out(igs, ig_send)

    @pl.when(owns)
    def _():
        wait_out(gpart.at[pl.ds(0, owners - 1)], rs_send)
        wait_out(agd.at[pl.ds(0, nz - 1)], ag_send)

    @pl.when(jnp.logical_not(owns))
    def _():
        wait_out(gpart, rs_send)

    wait_out(gres.at[ours], gx_send)
    wait_out(gmr.at[pl.ds(0, nz - 1)], gm_send)
    wait_out(gmx, gmx_send)


def hand_over(*refs):
    for i in range(5):
        refs[5 + i][...] = refs[i][...]


def per_device(nt, nz, hidden, tenant_ids, base_weight, adapter_in, adapter_out, magnitude, cotangent):
    tok, ffl = hidden.shape
    adapt = adapter_in.shape[1]
    tenants = magnitude.shape[0]
    rank = adapt // tenants
    tiles = (ffl // 128 + 2) * (rank // 8)
    per = 2
    owners = tiles // per
    vmem = pl.BlockSpec(memory_space=pltpu.VMEM)
    hbm = pl.BlockSpec(memory_space=pl.ANY)
    dma = pltpu.SemaphoreType.DMA
    tile = (8, 128)
    scratch = [
        pltpu.VMEM((ffl, adapt), bf16),
        pltpu.VMEM((adapt, 256), bf16),
        pltpu.VMEM((tenants, 256), f32),
        pltpu.VMEM((tok, 256), bf16),
        pltpu.VMEM((nz, ffl, 128), bf16),
        pltpu.VMEM((2, tok, ffl), bf16),
        pltpu.VMEM((adapt, 128), bf16),
        pltpu.VMEM((nt, adapt, 128), bf16),
        pltpu.VMEM((rank, tok), bf16),
        pltpu.VMEM((nt, rank, tok), bf16),
        pltpu.VMEM((rank, tok), bf16),
        pltpu.VMEM((nt, rank, tok), bf16),
        pltpu.VMEM(tile, f32),
        pltpu.VMEM((2 * nz,) + tile, f32),
        pltpu.VMEM(tile, f32),
        pltpu.VMEM((2,) + tile, f32),
        pltpu.VMEM((tok, 256), bf16),
        pltpu.VMEM((nt, tok, 256), bf16),
        pltpu.VMEM((nz, tok, 128), f32),
        pltpu.VMEM((nz, tok, 128), bf16),
        pltpu.VMEM((nz, tok, 128), bf16),
        pltpu.VMEM((nz, tok, 128), bf16),
        pltpu.VMEM((nt, tok, 128), bf16),
        pltpu.VMEM((2, tok, ffl), f32),
        pltpu.VMEM((tok, ffl), bf16),
        pltpu.VMEM((tok, ffl), bf16),
        pltpu.VMEM((owners, 8 * per, 128), bf16),
        pltpu.VMEM((2 * nz, 8 * per, 128), bf16),
        pltpu.VMEM((owners, tenants * per * 8, 128), bf16),
        pltpu.VMEM((nz, tenants * per * 8, 128), bf16),
        pltpu.VMEM((adapt, ffl), f32),
        pltpu.VMEM(tile, f32),
        pltpu.VMEM((nz,) + tile, f32),
        pltpu.VMEM(tile, f32),
        pltpu.VMEM(tile, f32),
        dma((6,)), dma, dma((nz,)), dma((nz,)), dma, dma, dma, dma,
        dma, dma, dma, dma, dma, dma, dma, dma((2,)),
        dma, dma((nt,)), dma, dma, dma((nz,)), dma, dma, dma, dma,
        dma, dma, dma, dma, dma, dma, dma, dma, dma, dma,
    ]
    results = pl.pallas_call(
        functools.partial(kernel, nt=nt, nz=nz),
        out_shape=(
            jax.ShapeDtypeStruct((tok, 256), bf16),
            jax.ShapeDtypeStruct((tok, ffl), bf16),
            jax.ShapeDtypeStruct((ffl, adapt), f32),
            jax.ShapeDtypeStruct((adapt, 256), f32),
            jax.ShapeDtypeStruct(magnitude.shape, f32),
        ),
        in_specs=[hbm, pl.BlockSpec(memory_space=pltpu.SMEM)] + [hbm] * 5,
        out_specs=[vmem] * 5,
        scratch_shapes=scratch,
        compiler_params=pltpu.CompilerParams(
            collective_id=0, has_side_effects=True, vmem_limit_bytes=63 * 2**20
        ),
        name="dora",
    )(hidden, tenant_ids, base_weight, adapter_in, adapter_out, magnitude, cotangent)
    return pl.pallas_call(
        hand_over,
        out_shape=[jax.ShapeDtypeStruct(r.shape, r.dtype) for r in results],
        in_specs=[vmem] * 5,
        out_specs=[vmem] * 5,
        compiler_params=pltpu.CompilerParams(vmem_limit_bytes=63 * 2**20),
        name="hand_over",
    )(*results)


def solution(mesh):
    nt = mesh.shape["tensor"]
    nz = mesh.shape["dp"] // 2
    return jax.shard_map(
        functools.partial(per_device, nt, nz),
        mesh=mesh,
        in_specs=(
            P("dp", "tensor"),
            P(),
            P("tensor", "dp"),
            P("tensor", None),
            P(None, "tensor"),
            P(None, "tensor"),
            P("dp", "tensor"),
        ),
        out_specs=(
            P("dp", "tensor"),
            P("dp", "tensor"),
            P("tensor", None),
            P(None, "tensor"),
            P(None, "tensor"),
        ),
        check_vma=False,
    )
```
